128 devices in a mesh: atoms: 32 (over y, x, core), kvec: 4 (over z).
Axes of the slice: x: 4, y: 4, z: 4, core: 2. Of those that a mesh axis runs over, the one named last changes fastest.
Arguments:
- positions: float32 [3, 16384], P(None, 'atoms'), as said below
- features: float32 [64, 16384], P(None, 'atoms'), may hold values from -6 to 6
- filter_one: float32 [16, 64], replicated, may hold values from -0.75 to 0.75
- filter_two: float32 [16, 64], replicated, may hold values from -0.75 to 0.75
- readout_in: float32 [64, 64], replicated, may hold values from -0.75 to 0.75
- readout_out: float32 [64], replicated, may hold values from -0.75 to 0.75
- charge_weight: float32 [64, 16], replicated, may hold values from -0.75 to 0.75
- neighbour_blocks: int32 [128, 9], P('atoms'), may hold values from 0 to 127, as said below
- live_slots: int32 [128], P('atoms'), may hold values from 4 to 9
- wave_ints: int32 [3, 8192], P(None, 'kvec'), may hold values from -16 to 56, as said below
Outputs:
- forces: float32 [3, 16384], P(None, 'atoms')
The draws below stay inside these ranges and needn't reach their ends.
Inputs may be any that keep to these rules, and one draw needn't show every extreme that they name: `neighbour_blocks`: slot 0 of row b is b; slots 1 to live_slots[b] - 1 list different blocks other than b, each on the same index of atoms as b or on one next to it, blocks being numbered 4 to an index in order; the remaining slots repeat b. `positions`: atoms of index p of atoms lie in x between 5 p and 5 p + 5 and in y between 0 and 10; the atoms of one block lie within a z range of length 128 / 5. `wave_ints`: the 8192 triples are different and nonzero; each has a positive first entry, or a zero first entry and a positive second, or zero first and second entries and a positive third; the second entry lies within -4 and 4.
All inputs are finite; a program needn't handle non-finite values.
Results may differ from the reference program's by a relative error of at most 0.0003.
Values sent between devices are 32-bit elements; how exact they have to be, the bound alone decides.
A program may use at most 64 MiB of HBM per device.

```python
import math
import jax
import jax.numpy as jnp
from jax import lax

F = 64
M = 16
Q = 16
BS = 128
NB = 9
BLK_DEV = 4
K = 8192
ATOMS = 16384
N_ATOMS = 32


def strip_order(key):
    key = jax.random.fold_in(key, 7)
    row_keys = jax.random.split(key, N_ATOMS)
    return jax.vmap(lambda row_key: jax.random.permutation(row_key, BLK_DEV))(row_keys).astype(jnp.int32)


def neighbour_table(key):
    strips = strip_order(key)
    inverse = jnp.argsort(strips, axis=1).astype(jnp.int32)
    block_total = BLK_DEV * N_ATOMS
    own_block = jnp.arange(block_total, dtype=jnp.int32)
    device_number = own_block // BLK_DEV
    strip_number = strips.reshape(-1)
    step_device = jnp.array([-1, -1, -1, 0, 0, 1, 1, 1], jnp.int32)
    step_strip = jnp.array([-1, 0, 1, -1, 1, -1, 0, 1], jnp.int32)
    other_device = device_number[:, None] + step_device[None, :]
    other_strip = strip_number[:, None] + step_strip[None, :]
    valid = (other_device >= 0) & (other_device < N_ATOMS) & (other_strip >= 0) & (other_strip < BLK_DEV)
    device_clipped = jnp.clip(other_device, 0, N_ATOMS - 1)
    strip_clipped = jnp.clip(other_strip, 0, BLK_DEV - 1)
    other_block = device_clipped * BLK_DEV + inverse[device_clipped, strip_clipped]
    other_block = jnp.where(valid, other_block, own_block[:, None])
    order_key = jax.random.fold_in(key, 8)
    row_keys = jax.random.split(order_key, block_total)
    ranking = jax.vmap(lambda row_key: jax.random.permutation(row_key, 8))(row_keys).astype(jnp.int32)
    scores = ranking + (1 - valid.astype(jnp.int32)) * 8
    picked = jnp.argsort(scores, axis=1, stable=True)
    ordered = jnp.take_along_axis(other_block, picked, axis=1)
    table = jnp.concatenate([own_block[:, None], ordered], axis=1).astype(jnp.int32)
    live = (1 + jnp.sum(valid.astype(jnp.int32), axis=1)).astype(jnp.int32)
    return (table, live)


def draw_positions(key, part):
    strips = strip_order(key)
    key = jax.random.fold_in(key, 11)
    per_device = BLK_DEV * BS
    total_atoms = per_device * N_ATOMS
    uniform_part = jax.random.uniform(key, (3, total_atoms), jnp.float32)
    slab_number = (jnp.arange(total_atoms) // per_device).astype(jnp.float32)
    strip_of_atom = jnp.repeat(strips.reshape(-1), BS).astype(jnp.float32)
    strip_length = BS / 5.0
    along_slab = (slab_number + uniform_part[0]) * 5.0
    across = uniform_part[1] * 10.0
    depth = (strip_of_atom + uniform_part[2]) * strip_length
    return jnp.stack([along_slab, across, depth], 0)


def draw_neighbour_blocks(key, part):
    table, live = neighbour_table(key)
    return table


def draw_live_slots(key, part):
    table, live = neighbour_table(key)
    return live


def draw_wave_ints(key, part):
    key = jax.random.fold_in(key, 14)
    span_first = 2 * K // 297 + 2
    count = span_first * 297
    index = jnp.arange(count, dtype=jnp.int32)
    first = index // 297
    rest = index % 297
    second = rest // 33 - 4
    third = rest % 33 - 16
    valid = (first > 0) | (second > 0) | (second == 0) & (third > 0)
    special = (first == span_first - 1) & (second == 0) & (third == 16) | (first == 1) & (second == 0) & (third == -16)
    ranking = jax.random.permutation(key, count).astype(jnp.int32)
    scores = jnp.where(special, -1, ranking) + (1 - valid.astype(jnp.int32)) * (count + 2)
    picked = jnp.argsort(scores, stable=True)[:K]
    triples = jnp.stack([first, second, third], 0)
    return jnp.take(triples, picked, axis=1).astype(jnp.int32)


def block_scale(own_key, extent, cuts, low, largest):
    loudness = 1.0
    for position, shards_of in cuts:
        steps = jax.random.uniform(jax.random.fold_in(jax.random.fold_in(own_key, 6), position), (shards_of,), jnp.float32, low / len(cuts), largest / len(cuts))
        loudness = loudness * jnp.repeat(jnp.exp(steps), extent[position] // shards_of).reshape((-1,) + (1,) * (len(extent) - 1 - position))
    return loudness


def gaussian(key, shape, width, bound, shards=(), kind=jnp.bfloat16):
    gain = block_scale(key, shape, shards, -0.22, 0.18) if shards else 1.0
    drawn = jax.random.normal(key, shape, jnp.float32) * width * gain
    return jnp.minimum(jnp.maximum(drawn, -bound), bound).astype(kind)


def setup_inputs(seed: int = 0) -> dict:
    splits = jax.random.split(jax.random.key(seed), 11)
    positions = draw_positions(jax.random.fold_in(splits[10], 71), 0)
    features = gaussian(splits[1], (F, ATOMS), 1.0, 6.0, ((1, 32),), jnp.float32)
    filter_one = gaussian(splits[2], (M, F), (M * 4) ** -0.5, 0.75, (), jnp.float32)
    filter_two = gaussian(splits[3], (M, F), (M * 4) ** -0.5, 0.75, (), jnp.float32)
    readout_in = gaussian(splits[4], (F, F), F ** -0.5, 0.75, (), jnp.float32)
    readout_out = gaussian(splits[5], (F,), F ** -0.5, 0.75, (), jnp.float32)
    charge_weight = gaussian(splits[6], (F, Q), F ** -0.5, 0.75, (), jnp.float32)
    neighbour_blocks = draw_neighbour_blocks(jax.random.fold_in(splits[10], 71), 0)
    live_slots = draw_live_slots(jax.random.fold_in(splits[10], 71), 0)
    wave_ints = draw_wave_ints(jax.random.fold_in(splits[10], 71), 0)
    return dict(positions=positions, features=features, filter_one=filter_one, filter_two=filter_two, readout_in=readout_in, readout_out=readout_out, charge_weight=charge_weight, neighbour_blocks=neighbour_blocks, live_slots=live_slots, wave_ints=wave_ints)


highest = lax.Precision.HIGHEST
slab_width = 5.0
slab_height = 10.0
atom_density = 0.1
cutoff_radius = 5.0
self_offset = 0.0001
screen_square = 0.25
spread_square = 1.0

def radial(distance, basis_count):
    steps_along = jnp.arange(basis_count).astype(jnp.float32)
    centers = cutoff_radius * steps_along / (basis_count - 1)
    sharpness = 0.5 * ((basis_count - 1) / cutoff_radius) ** 2
    envelope = jnp.where(distance < cutoff_radius, 0.5 * (jnp.cos(jnp.pi * distance / cutoff_radius) + 1.0), 0.0)
    shaped = centers.reshape((basis_count,) + (1,) * distance.ndim)
    return envelope[None] * jnp.exp(-sharpness * (distance[None] - shaped) ** 2)

def block_messages(centre, near_pos, near_val, live_row, filter_pair):
    block_size = centre.shape[1]
    slot_count = near_pos.shape[1]
    basis_count = filter_pair.shape[0]
    offset = centre[:, :, None, None] - near_pos[:, None, :, :]
    distance = jnp.sqrt(lax.optimization_barrier(jnp.sum(offset * offset, axis=0)) + self_offset)
    atom_left = jnp.arange(block_size)[:, None, None]
    atom_right = jnp.arange(block_size)[None, None, :]
    slot_number = jnp.arange(slot_count)[None, :, None]
    active = live_row[None, :, None] & ((slot_number > 0) | (atom_left != atom_right))
    radial_terms = radial(distance, basis_count) * active[None].astype(distance.dtype)
    radial_terms = radial_terms.reshape(basis_count, block_size, slot_count * block_size)
    values = near_val.reshape(near_val.shape[0], slot_count * block_size)
    gathered = jnp.einsum('mij,fj->mfi', radial_terms, values, precision=highest)
    return jnp.einsum('mf,mfi->fi', filter_pair, gathered, precision=highest)

def messages(own_pos, wide_pos, wide_values, filter_pair, near_ids, live_mask):
    block_count = near_ids.shape[0]
    block_size = own_pos.shape[1] // block_count
    own_blocks = own_pos.reshape(3, block_count, block_size)
    pos_blocks = wide_pos.reshape(3, -1, block_size)
    value_blocks = wide_values.reshape(wide_values.shape[0], -1, block_size)

    def per_block(block_index):
        chosen = near_ids[block_index]
        centre = lax.dynamic_index_in_dim(own_blocks, block_index, 1, keepdims=False)
        near_pos = jnp.take(pos_blocks, chosen, axis=1)
        near_val = jnp.take(value_blocks, chosen, axis=1)
        return block_messages(centre, near_pos, near_val, live_mask[block_index], filter_pair)
    result = lax.map(jax.checkpoint(per_block), jnp.arange(block_count, dtype=jnp.int32))
    return jnp.transpose(result, (1, 0, 2)).reshape(wide_values.shape[0], -1)

def readout_energy(values, readout_in, readout_out):
    hidden = jnp.dot(readout_in.T, values, precision=highest)
    return jnp.sum(jax.nn.silu(hidden) * readout_out[:, None])

def wave_table(wave_ints, device_count, local_atoms):
    depth_side = local_atoms / (atom_density * slab_width * slab_height)
    scales = jnp.array([2.0 * math.pi / (slab_width * device_count), 2.0 * math.pi / slab_height, 2.0 * math.pi / depth_side], jnp.float32)
    waves = wave_ints.astype(jnp.float32) * scales[:, None]
    squared = lax.optimization_barrier(jnp.sum(waves * waves, axis=0))
    return (waves, jnp.exp(-0.5 * spread_square * squared) / (squared + screen_square))

def reference(positions, features, filter_one, filter_two, readout_in, readout_out, charge_weight, neighbour_blocks, live_slots, wave_ints):
    live_mask = jnp.arange(NB)[None, :] < live_slots[:, None]
    waves, wave_weight = wave_table(wave_ints, N_ATOMS, BLK_DEV * BS)
    wave_block = math.gcd(K, 512)
    wave_groups = jnp.transpose(waves.reshape(3, K // wave_block, wave_block), (1, 0, 2))
    weight_groups = wave_weight.reshape(K // wave_block, wave_block)

    def energy(coords):
        z_one = features + messages(coords, coords, features, filter_one, neighbour_blocks, live_mask)
        z_two = z_one + messages(coords, coords, z_one, filter_two, neighbour_blocks, live_mask)
        short = readout_energy(z_two, readout_in, readout_out)
        charges = jnp.dot(charge_weight.T, z_two, precision=highest)

        def per_wave(pair):
            group, group_weight = pair
            phases = jnp.dot(group.T, coords, precision=highest)
            cosine_sum = jnp.dot(charges, jnp.cos(phases).T, precision=highest)
            sine_sum = jnp.dot(charges, jnp.sin(phases).T, precision=highest)
            return jnp.sum(group_weight[None, :] * (cosine_sum * cosine_sum + sine_sum * sine_sum))
        longer = jnp.sum(lax.map(jax.checkpoint(per_wave), (wave_groups, weight_groups)))
        return short + longer / ATOMS
    return -jax.grad(energy)(positions)
```

```python
import functools
import math

import jax
import jax.numpy as jnp
import numpy as np
from jax import lax
from jax.experimental import pallas as pl
from jax.experimental.pallas import tpu as pltpu
from jax.sharding import PartitionSpec as P

MESH = pl.DeviceIdType.MESH
highest = lax.Precision.HIGHEST
f32 = jnp.float32
bf16 = jnp.bfloat16
slab_width = 5.0
slab_height = 10.0
atom_density = 0.1
cutoff_radius = 5.0
self_offset = 0.0001
screen_square = 0.25
spread_square = 1.0


def trig_coefficients():
    u = 0.5 * np.cos(np.pi * (np.arange(4000) + 0.5) / 8000)
    cheb = np.polynomial.chebyshev
    scaled = 8.0 * u * u - 1.0
    out = []
    for values, degree, weight in (
        (np.sin(2 * np.pi * u) / u, 6, u),
        (np.cos(2 * np.pi * u), 6, np.ones_like(u)),
    ):
        fitted = cheb.Chebyshev(cheb.chebfit(scaled, values, degree, w=weight))
        poly = fitted.convert(kind=np.polynomial.Polynomial)
        shifted = poly(np.polynomial.Polynomial([-1.0, 8.0]))
        out.append([float(c) for c in shifted.coef])
    return out


SIN_COEF, COS_COEF = trig_coefficients()


def sin_cos_turns(u):
    square = u * u
    sine = SIN_COEF[-1]
    for c in SIN_COEF[-2::-1]:
        sine = sine * square + c
    cosine = COS_COEF[-1]
    for c in COS_COEF[-2::-1]:
        cosine = cosine * square + c
    return sine * u, cosine


def split(x):
    high = x.astype(bf16)
    return high, (x - high.astype(f32)).astype(bf16)


def dot_nt(a, b):
    return lax.dot_general(a, b, (((1,), (1,)), ((), ())), preferred_element_type=f32)


def dot_nn(a, b):
    return lax.dot_general(a, b, (((1,), (0,)), ((), ())), preferred_element_type=f32)


def exact_nn(a, b):
    return lax.dot_general(
        a, b, (((1,), (0,)), ((), ())), precision=highest, preferred_element_type=f32
    )


def exact_tn(a, b):
    return lax.dot_general(
        a, b, (((0,), (0,)), ((), ())), precision=highest, preferred_element_type=f32
    )


def kernel(
    sizes,
    pos_ref, feat_ref, f1_ref, f2_ref, rin_ref, rout_ref, cw_ref, wave_ref, nb_ref, live_ref,
    out_ref,
    wide, zwide, post, xpad, own_t, nf, wtab, thi, tlo, ahi, alo, zf, zz, geo,
    wd1, wd2, wcol, gwt, gw, bbuf, qsum, tslot, tsend, trecv, qbuf, sfb, rsb, agb, rmat,
    cgs, cgr, wf, pg, fsend, frecv, inv,
    ssem, rsem, halo_r,
):
    n_at, n_k, n_blk, bs, n_slot, n_f, n_m, n_q, n_wave = sizes
    total_atoms = n_at * n_blk * bs
    p = lax.axis_index("atoms")
    q = lax.axis_index("kvec")
    half_m = n_m // 2
    wide_n = n_slot * bs
    k_chunks = n_wave // bs
    near_peers = [(dp, dq) for dp in (-1, 0, 1) for dq in range(n_k) if (dp, dq) != (0, 0)]

    def peer(dp, dq):
        return {"atoms": lax.rem(p + dp + n_at, n_at), "kvec": lax.rem(q + dq, n_k)}

    def send(src, dst, which, dp, dq, recv=None):
        copy = pltpu.make_async_remote_copy(
            src_ref=src, dst_ref=dst, send_sem=ssem.at[which],
            recv_sem=rsem.at[which] if recv is None else recv,
            device_id=peer(dp, dq), device_id_type=MESH,
        )
        copy.start()

    def wait_bytes(ref, sem):
        pltpu.make_async_copy(ref, ref, sem).wait()

    barrier = pltpu.get_barrier_semaphore()
    partners = near_peers + [(d, 0) for d in range(2, n_at - 1)]
    for dp, dq in partners:
        pl.semaphore_signal(barrier, inc=1, device_id=peer(dp, dq), device_id_type=MESH)

    for c in range(n_blk):
        lanes = slice(c * bs, (c + 1) * bs)
        wide[n_blk + c, 0:n_f, :] = feat_ref[:, lanes]
        wide[n_blk + c, n_f:, :] = jnp.zeros((8, bs), f32)
        wide[n_blk + c, n_f : n_f + 3, :] = pos_ref[:, lanes]
    pl.semaphore_wait(barrier, len(partners))
    own_rows = wide.at[pl.ds(n_blk, n_blk)]
    send(own_rows, wide.at[pl.ds(0, n_blk)], 0, 1, 0, halo_r.at[0])
    send(own_rows, wide.at[pl.ds(2 * n_blk, n_blk)], 0, -1, 0, halo_r.at[1])

    live = live_ref[q]
    base = (p - 1) * n_blk
    total_blocks = n_at * n_blk

    def near_id(s):
        return jnp.minimum(lax.rem(nb_ref[q, s] - base + total_blocks, total_blocks), 3 * n_blk - 1)

    near = [near_id(s) for s in range(n_slot)]
    for c in range(3 * n_blk):
        found = jnp.int32(n_slot)
        for s in range(n_slot - 1, -1, -1):
            found = jnp.where((near[s] == c) & (s < live), s, found)
        inv[c] = found

    xpad[...] = jnp.zeros((bs, bs), f32)
    for c in range(n_blk):
        xpad[0:3, :] = pos_ref[:, c * bs : (c + 1) * bs]
        post[c] = xpad[...].T
    own_t[...] = post[q]

    steps = lax.broadcasted_iota(jnp.int32, (n_m, 2 * n_f), 0).astype(f32) - half_m
    gain = jnp.exp(-0.5 * steps * steps)
    for wd, src in ((wd1, f1_ref), (wd2, f2_ref)):
        wd[...] = jnp.concatenate([src[...], src[...]], axis=1) * gain
    xpad[0:n_m, :] = wd2[...]
    wcol[...] = xpad[...].T

    nf[0:3, :] = wave_ref[...].astype(f32)
    depth_side = n_blk * bs / (atom_density * slab_width * slab_height)
    sides = (slab_width * n_at, slab_height, depth_side)
    scales = [2.0 * math.pi / side for side in sides]
    kx, ky, kz = (nf[a : a + 1, :] * scales[a] for a in range(3))
    square = kx * kx + ky * ky + kz * kz
    weight = jnp.exp(-0.5 * spread_square * square) / (square + screen_square) * (2.0 / total_atoms)
    for c in range(k_chunks):
        wtab[c, 0:1, :] = weight[:, c * bs : (c + 1) * bs]

    rows_t = 16
    span = min(n_wave, 512)

    def tables(block):
        def one(step, carry):
            at = pl.multiple_of(step * rows_t, rows_t)
            cols = []
            for a in range(3):
                col = post[block, pl.ds(at, rows_t), a : a + 1] * (1.0 / sides[a])
                cols.append(col - jnp.round(col))
            row = pl.ds(pl.multiple_of(block * bs + at, rows_t), rows_t)
            for start in range(0, n_wave, span):
                lanes = slice(start, start + span)
                u = cols[0] * nf[0:1, lanes] + cols[1] * nf[1:2, lanes] + cols[2] * nf[2:3, lanes]
                sine, cosine = sin_cos_turns(u - jnp.round(u))
                thi[row, lanes], tlo[row, lanes] = split(cosine)
                later = slice(n_wave + start, n_wave + start + span)
                thi[row, later], tlo[row, later] = split(sine)
            return carry

        lax.fori_loop(0, bs // rows_t, one, 0)

    for block in range(n_blk // 2):
        tables(block)

    wait_bytes(own_rows, halo_r.at[0])
    wait_bytes(own_rows, halo_r.at[1])

    rows_g = 32
    centre = cutoff_radius * half_m / (n_m - 1)
    spacing = cutoff_radius / (n_m - 1)
    sharp = 0.5 / spacing ** 2

    def put_values(dest, value, lanes):
        high, low = split(value)
        dest[0:n_f, lanes] = high
        dest[n_f : 2 * n_f, lanes] = low
        dest[2 * n_f : 3 * n_f, lanes] = high
        dest[3 * n_f : 4 * n_f, lanes] = low

    def pairs(s, carry):
        block = near_id(s)
        lanes = pl.ds(pl.multiple_of(s * bs, bs), bs)
        alive = jnp.where(s < live, 1.0, 0.0).astype(f32)
        put_values(zf, wide[block, 0:n_f, :], lanes)
        right = [wide[block, n_f + a : n_f + a + 1, :] for a in range(3)]
        for start in range(0, bs, rows_g):
            rows = slice(start, start + rows_g)
            dx, dy, dz = (own_t[rows, a : a + 1] - right[a] for a in range(3))
            squared = dx * dx + dy * dy + dz * dz + self_offset
            inverse = lax.rsqrt(squared)
            r = squared * inverse
            i = lax.broadcasted_iota(jnp.int32, (rows_g, bs), 0) + start
            j = lax.broadcasted_iota(jnp.int32, (rows_g, bs), 1)
            off = (i - j) * (i - j) + s
            active = jnp.where((r < cutoff_radius) & (off != 0), alive, 0.0)
            r = jnp.minimum(r, cutoff_radius)
            rho = r - centre
            bell = jnp.exp(-sharp * rho * rho)
            tau = jnp.exp((2.0 * sharp * spacing) * rho)
            tin = jnp.exp((-2.0 * sharp * spacing) * rho)
            sine, cosine = sin_cos_turns(r * (0.25 / cutoff_radius))
            cosine = cosine * active
            cut = cosine * cosine
            slope = (-math.pi / cutoff_radius) * sine * cosine
            first = cut * bell
            geo[0, rows, lanes] = dx
            geo[1, rows, lanes] = dy
            geo[2, rows, lanes] = dz
            geo[3, rows, lanes] = tau
            geo[4, rows, lanes] = tin
            geo[5, rows, lanes] = (slope - (2.0 * sharp) * rho * cut) * bell * inverse
            geo[6, rows, lanes] = (2.0 * sharp * spacing) * first * inverse
            term = first
            for m in range(half_m, n_m):
                out = slice(m * bs + start, m * bs + start + rows_g)
                ahi[out, lanes], alo[out, lanes] = split(term)
                term = term * tau
            term = first
            for m in range(half_m - 1, -1, -1):
                term = term * tin
                out = slice(m * bs + start, m * bs + start + rows_g)
                ahi[out, lanes], alo[out, lanes] = split(term)
        return carry

    lax.fori_loop(0, n_slot, pairs, 0)

    group = 4

    def messages(values, wd):
        total = jnp.zeros((bs, 2 * n_f), f32)
        stack = values[0 : 2 * n_f, :]
        for g in range(0, n_m, group):
            rows = slice(g * bs, (g + group) * bs)
            got = dot_nt(ahi[rows, :], stack) + dot_nt(alo[rows, :], stack)
            for m in range(group):
                total = total + got[m * bs : (m + 1) * bs] * wd[g + m : g + m + 1, :]
        flipped = total.T
        return flipped[0:n_f] + flipped[n_f:]

    z_one = wide[n_blk + q, 0:n_f, :] + messages(zf, wd1)
    mine = n_blk + q
    zwide[mine] = z_one
    for dp, dq in near_peers:
        send(zwide.at[mine], zwide.at[(1 - dp) * n_blk + q], 1, dp, dq)
    for block in range(n_blk // 2, n_blk):
        tables(block)
    wait_bytes(zwide.at[pl.ds(0, 3 * n_blk - 1)], rsem.at[1])
    for s in range(n_slot):
        put_values(zz, zwide[near[s]], slice(s * bs, (s + 1) * bs))
    z_two = z_one + messages(zz, wd2)

    qbuf[q] = exact_tn(cw_ref[...], z_two)
    for dq in range(1, n_k):
        send(qbuf.at[q], qbuf.at[q], 2, 0, dq)
    hidden = exact_tn(rin_ref[...], z_two)
    gate = 1.0 / (1.0 + jnp.exp(-hidden))
    bent = gate * (1.0 + hidden * (1.0 - gate))
    short_grad = exact_nn(rin_ref[...] * rout_ref[...], bent)
    wait_bytes(qbuf.at[pl.ds(0, n_k - 1)], rsem.at[2])

    charges = jnp.concatenate([qbuf[c] for c in range(n_blk)], axis=1)
    stacked = jnp.concatenate(split(charges), axis=0)
    got = dot_nn(stacked, thi[...]) + dot_nn(stacked, tlo[...])
    got = got[0:n_q] + got[n_q:]
    for c in range(2 * k_chunks):
        sfb[c] = got[:, c * bs : (c + 1) * bs]
    for d in range(1, n_at):
        send(sfb.at[lax.rem(p + d, n_at)], rsb.at[d - 1], 3, d, 0)
    wait_bytes(rsb, rsem.at[3])
    part = sfb[p]
    for d in range(n_at - 1):
        part = part + rsb[d]
    agb[p] = part * wtab[lax.rem(p, k_chunks), 0:1, :]
    for d in range(1, n_at):
        send(agb.at[p], agb.at[p], 4, d, 0)
    wait_bytes(agb.at[pl.ds(0, n_at - 1)], rsem.at[4])

    for c in range(k_chunks):
        cos_part, sin_part = agb[c], agb[k_chunks + c]
        lanes = slice(c * bs, (c + 1) * bs)
        later = slice(n_wave + c * bs, n_wave + (c + 1) * bs)
        rows = [cos_part] + [sin_part * (nf[a : a + 1, lanes] * scales[a]) for a in range(3)]
        rows2 = [sin_part] + [cos_part * (nf[a : a + 1, lanes] * -scales[a]) for a in range(3)]
        for place, pieces in ((lanes, rows), (later, rows2)):
            for a, piece in enumerate(pieces):
                high, low = split(piece)
                rmat[a * n_q : (a + 1) * n_q, place] = high
                rmat[(4 + a) * n_q : (5 + a) * n_q, place] = low
    got = dot_nt(thi[...], rmat[...]) + dot_nt(tlo[...], rmat[...])
    folded = []
    for c in range(n_blk):
        flipped = got[c * bs : (c + 1) * bs].T
        flipped = flipped[0 : 4 * n_q] + flipped[4 * n_q :]
        cgs[c] = flipped[0:n_q]
        folded.append(flipped)
    for dq in range(1, n_k):
        send(cgs.at[lax.rem(q + dq, n_k)], cgr.at[dq - 1], 5, 0, dq)
    for c in range(n_blk):
        for a in range(3):
            product = qbuf[c] * folded[c][(1 + a) * n_q : (2 + a) * n_q]
            wf[a : a + 1, c * bs : (c + 1) * bs] = jnp.sum(product, axis=0, keepdims=True)
    wait_bytes(cgr, rsem.at[5])
    charge_grad = cgs[q] + cgr[0]
    for dq in range(1, n_k - 1):
        charge_grad = charge_grad + cgr[dq]
    g_two = exact_nn(cw_ref[...], charge_grad) + short_grad

    for m in range(n_m):
        lanes = slice(m * bs, (m + 1) * bs)
        high, low = split(g_two * wcol[0:n_f, m : m + 1])
        gwt[0:n_f, lanes] = high
        gwt[n_f:, lanes] = low
    got = dot_nn(gwt[...], ahi[...]) + dot_nn(gwt[...], alo[...])
    got = got[0:n_f] + got[n_f:]
    for s in range(n_slot):
        tslot[s] = got[:, s * bs : (s + 1) * bs]
    tslot[n_slot] = jnp.zeros((n_f, bs), f32)
    for index, (dp, dq) in enumerate(near_peers):
        block = (1 + dp) * n_blk + lax.rem(q + dq, n_k)
        tsend[index] = tslot[inv[block]]
        send(tsend.at[index], trecv.at[index], 6, dp, dq)

    def pair_sums(grad, wd, values, last):
        twice = jnp.concatenate([grad, grad], axis=0).T
        for m in range(n_m):
            rows = slice(m * bs, (m + 1) * bs)
            high, low = split(twice * wd[m : m + 1, :])
            gw[rows, 0 : 2 * n_f] = high
            gw[rows, 2 * n_f :] = low
        rows_h = 16
        for tile, start in enumerate(range(0, wide_n, 2 * bs)):
            width = min(2 * bs, wide_n - start)
            lanes = slice(start, start + width)
            buf = tile % 2
            bbuf[buf, :, 0:width] = dot_nn(gw[...], values[:, lanes])

            def horner(step, carry):
                at = pl.multiple_of(step * rows_h, rows_h)
                rows = pl.ds(at, rows_h)

                def term(m):
                    here = pl.ds(pl.multiple_of(m * bs + at, rows_h), rows_h)
                    return bbuf[buf, here, 0:width]

                tau = geo[3, rows, lanes]
                up = term(n_m - 1)
                up_d = up
                for m in range(n_m - 2, half_m, -1):
                    up = up * tau + term(m)
                    up_d = up_d * tau + up
                up = up * tau + term(half_m)
                tin = geo[4, rows, lanes]
                down = term(0)
                down_d = down
                for m in range(1, half_m):
                    down = down * tin + term(m)
                    down_d = down_d * tin + down
                zero_sum = up + down * tin
                one_sum = up_d * tau - down_d * tin
                value = geo[5, rows, lanes] * zero_sum + geo[6, rows, lanes] * one_sum
                if last:
                    value = value + qsum[rows, lanes]
                qsum[rows, lanes] = value
                return carry

            lax.fori_loop(0, bs // rows_h, horner, 0)

    pair_sums(g_two, wd2, zz, False)
    wait_bytes(trecv, rsem.at[6])
    g_one = g_two + tslot[0]
    for index in range(len(near_peers)):
        g_one = g_one + trecv[index]
    pair_sums(g_one, wd1, zf, True)

    own = [jnp.zeros((bs, bs), f32) for _ in range(3)]
    for s in range(n_slot):
        lanes = slice(s * bs, (s + 1) * bs)
        value = qsum[:, lanes]
        for a in range(3):
            product = value * geo[a, :, lanes]
            own[a] = own[a] + product
            pg[s, a : a + 1, :] = -jnp.sum(product, axis=0, keepdims=True)
    pg[n_slot, 0:3, :] = jnp.zeros((3, bs), f32)
    for a in range(3):
        pg[0, a : a + 1, :] = pg[0, a : a + 1, :] + jnp.sum(own[a].T, axis=0, keepdims=True)
    fsend[...] = jnp.zeros(fsend.shape, f32)
    for side in range(3):
        for c in range(n_blk):
            lanes = slice(c * bs, (c + 1) * bs)
            value = pg[inv[side * n_blk + c], 0:3, :]
            if side == 1:
                value = value + wf[0:3, lanes]
            fsend[side, 0:3, lanes] = value
    for index, (dp, dq) in enumerate(near_peers):
        send(fsend.at[1 + dp], frecv.at[index], 7, dp, dq)
    wait_bytes(frecv, rsem.at[7])
    force = fsend[1, 0:3, :]
    for index in range(len(near_peers)):
        force = force + frecv[index, 0:3, :]
    out_ref[...] = -force

    wait_bytes(wide.at[pl.ds(0, 2 * n_blk)], ssem.at[0])
    wait_bytes(zwide.at[pl.ds(0, 3 * n_blk - 1)], ssem.at[1])
    wait_bytes(qbuf.at[pl.ds(0, n_k - 1)], ssem.at[2])
    wait_bytes(rsb, ssem.at[3])
    wait_bytes(agb.at[pl.ds(0, n_at - 1)], ssem.at[4])
    wait_bytes(cgr, ssem.at[5])
    wait_bytes(trecv, ssem.at[6])
    wait_bytes(frecv, ssem.at[7])


def body(
    n_at, n_k,
    positions, features, filter_one, filter_two, readout_in, readout_out, charge_weight,
    neighbour_blocks, live_slots, wave_ints,
):
    n_f = features.shape[0]
    n_m = filter_one.shape[0]
    n_q = charge_weight.shape[1]
    n_blk, n_slot = neighbour_blocks.shape
    bs = positions.shape[1] // n_blk
    n_wave = wave_ints.shape[1]
    local = n_blk * bs
    wide_n = n_slot * bs
    near_n = 3 * n_blk - 1
    k_chunks = n_wave // bs
    sizes = (n_at, n_k, n_blk, bs, n_slot, n_f, n_m, n_q, n_wave)
    v = pltpu.VMEM
    scratch = [
        v((3 * n_blk, n_f + 8, bs), f32),
        v((3 * n_blk, n_f, bs), f32),
        v((n_blk, bs, bs), f32),
        v((bs, bs), f32),
        v((bs, bs), f32),
        v((8, n_wave), f32),
        v((k_chunks, 8, bs), f32),
        v((local, 2 * n_wave), bf16),
        v((local, 2 * n_wave), bf16),
        v((n_m * bs, wide_n), bf16),
        v((n_m * bs, wide_n), bf16),
        v((4 * n_f, wide_n), bf16),
        v((4 * n_f, wide_n), bf16),
        v((7, bs, wide_n), f32),
        v((n_m, 2 * n_f), f32),
        v((n_m, 2 * n_f), f32),
        v((bs, bs), f32),
        v((2 * n_f, n_m * bs), bf16),
        v((n_m * bs, 4 * n_f), bf16),
        v((2, n_m * bs, 2 * bs), f32),
        v((bs, wide_n), f32),
        v((n_slot + 1, n_f, bs), f32),
        v((near_n, n_f, bs), f32),
        v((near_n, n_f, bs), f32),
        v((n_k, n_q, bs), f32),
        v((n_at, n_q, bs), f32),
        v((n_at - 1, n_q, bs), f32),
        v((n_at, n_q, bs), f32),
        v((8 * n_q, 2 * n_wave), bf16),
        v((n_blk, n_q, bs), f32),
        v((n_k - 1, n_q, bs), f32),
        v((8, local), f32),
        v((n_slot + 1, 8, bs), f32),
        v((3, 8, local), f32),
        v((near_n, 8, local), f32),
        pltpu.SMEM((3 * n_blk,), jnp.int32),
        pltpu.SemaphoreType.DMA((8,)),
        pltpu.SemaphoreType.DMA((8,)),
        pltpu.SemaphoreType.DMA((2,)),
    ]
    vmem = pl.BlockSpec(memory_space=pltpu.VMEM)
    smem = pl.BlockSpec(memory_space=pltpu.SMEM)
    return pl.pallas_call(
        functools.partial(kernel, sizes),
        out_shape=jax.ShapeDtypeStruct(positions.shape, f32),
        in_specs=[vmem] * 8 + [smem] * 2,
        out_specs=vmem,
        scratch_shapes=scratch,
        compiler_params=pltpu.CompilerParams(
            collective_id=0, has_side_effects=True, vmem_limit_bytes=56 * 2**20
        ),
    )(
        positions, features, filter_one, filter_two, readout_in,
        readout_out.reshape(1, n_f), charge_weight, wave_ints, neighbour_blocks, live_slots,
    )


def solution(mesh):
    in_specs = (
        P(None, "atoms"), P(None, "atoms"), P(), P(), P(), P(), P(),
        P("atoms", None), P("atoms"), P(None, "kvec"),
    )
    return jax.shard_map(
        functools.partial(body, mesh.shape["atoms"], mesh.shape["kvec"]),
        mesh=mesh, in_specs=in_specs, out_specs=P(None, "atoms"), check_vma=False,
    )
```

```python
import functools
import math

import jax
import jax.numpy as jnp
import numpy as np
from jax import lax
from jax.experimental import pallas as pl
from jax.experimental.pallas import tpu as pltpu
from jax.sharding import PartitionSpec as P

MESH = pl.DeviceIdType.MESH
highest = lax.Precision.HIGHEST
f32 = jnp.float32
bf16 = jnp.bfloat16
slab_width = 5.0
slab_height = 10.0
atom_density = 0.1
cutoff_radius = 5.0
self_offset = 0.0001
screen_square = 0.25
spread_square = 1.0
n_group = 8


def trig_coefficients():
    u = 0.5 * np.cos(np.pi * (np.arange(4000) + 0.5) / 8000)
    cheb = np.polynomial.chebyshev
    scaled = 8.0 * u * u - 1.0
    out = []
    for values, degree, weight in (
        (np.sin(2 * np.pi * u) / u, 6, u),
        (np.cos(2 * np.pi * u), 6, np.ones_like(u)),
    ):
        fitted = cheb.Chebyshev(cheb.chebfit(scaled, values, degree, w=weight))
        poly = fitted.convert(kind=np.polynomial.Polynomial)
        shifted = poly(np.polynomial.Polynomial([-1.0, 8.0]))
        out.append([float(c) for c in shifted.coef])
    return out


SIN_COEF, COS_COEF = trig_coefficients()


def sin_cos_turns(u):
    square = u * u
    sine = SIN_COEF[-1]
    for c in SIN_COEF[-2::-1]:
        sine = sine * square + c
    cosine = COS_COEF[-1]
    for c in COS_COEF[-2::-1]:
        cosine = cosine * square + c
    return sine * u, cosine


def split(x):
    high = x.astype(bf16)
    return high, (x - high.astype(f32)).astype(bf16)


def dot_nt(a, b):
    return lax.dot_general(a, b, (((1,), (1,)), ((), ())), preferred_element_type=f32)


def dot_nn(a, b):
    return lax.dot_general(a, b, (((1,), (0,)), ((), ())), preferred_element_type=f32)


def exact_nn(a, b):
    return lax.dot_general(
        a, b, (((1,), (0,)), ((), ())), precision=highest, preferred_element_type=f32
    )


def exact_tn(a, b):
    return lax.dot_general(
        a, b, (((0,), (0,)), ((), ())), precision=highest, preferred_element_type=f32
    )


def kernel(
    sizes,
    pos_ref, feat_ref, f1_ref, f2_ref, rin_ref, rout_ref, cw_ref, wave_ref, nb_ref, live_ref,
    out_ref,
    wide, zwide, post, xpad, own_t, nf, wtab, thi, tlo, ahi, alo, zf, zz, geo,
    wd1, wd2, wcol, gwt, gw, buf_a, buf_b, qsum, tslot, tsend, trecv, qbuf, sfb, rsb, agb, agpart, rmat,
    cgs, cgr, wf, pg, fsend, frecv, inv,
    ssem, rsem, halo_r, group_r, greet_sem,
):
    n_at, n_k, n_blk, bs, n_slot, n_f, n_m, n_q, n_wave = sizes
    total_atoms = n_at * n_blk * bs
    p = lax.axis_index("atoms")
    q = lax.axis_index("kvec")
    half_m = n_m // 2
    wide_n = n_slot * bs
    wide_p = zf.shape[1]
    k_chunks = n_wave // bs
    across = [(0, dq) for dq in range(1, n_k)]
    beside = [(1, 0), (-1, 0)]
    near_peers = [(dp, dq) for dq in range(1, n_k) for dp in (1, -1)] + across + beside

    def peer(dp, dq):
        return {"atoms": lax.rem(p + dp + n_at, n_at), "kvec": lax.rem(q + dq, n_k)}

    def send(src, dst, which, dp, dq, recv=None):
        copy = pltpu.make_async_remote_copy(
            src_ref=src, dst_ref=dst, send_sem=ssem.at[which],
            recv_sem=rsem.at[which] if recv is None else recv,
            device_id=peer(dp, dq), device_id_type=MESH,
        )
        copy.start()

    def wait_bytes(ref, sem):
        pltpu.make_async_copy(ref, ref, sem).wait()

    barrier = pltpu.get_barrier_semaphore()
    partners = across + beside
    for dp, dq in partners:
        pl.semaphore_signal(barrier, inc=1, device_id=peer(dp, dq), device_id_type=MESH)

    def greet(index, group):
        for dp, dq in group:
            pl.semaphore_signal(
                greet_sem.at[index], inc=1, device_id=peer(dp, dq), device_id_type=MESH
            )

    def met(index, group):
        pl.semaphore_wait(greet_sem.at[index], len(group))

    rounds = []
    reach = 1
    while reach < n_at // 2:
        rounds.append([(reach, 0), (-reach, 0)])
        reach *= 2

    for c in range(n_blk):
        lanes = slice(c * bs, (c + 1) * bs)
        wide[n_blk + c, 0:n_f, :] = feat_ref[:, lanes]
        wide[n_blk + c, n_f:, :] = jnp.zeros((8, bs), f32)
        wide[n_blk + c, n_f : n_f + 3, :] = pos_ref[:, lanes]
    pl.semaphore_wait(barrier, len(partners))
    own_rows = wide.at[pl.ds(n_blk, n_blk)]
    send(own_rows, wide.at[pl.ds(0, n_blk)], 0, 1, 0, halo_r.at[0])
    send(own_rows, wide.at[pl.ds(2 * n_blk, n_blk)], 0, -1, 0, halo_r.at[1])
    greet(0, across)
    greet(1, rounds[0])

    live = live_ref[q]
    base = (p - 1) * n_blk
    total_blocks = n_at * n_blk

    def near_id(s):
        return jnp.minimum(lax.rem(nb_ref[q, s] - base + total_blocks, total_blocks), 3 * n_blk - 1)

    near = [near_id(s) for s in range(n_slot)]
    for c in range(3 * n_blk):
        found = jnp.int32(n_slot)
        for s in range(n_slot - 1, -1, -1):
            found = jnp.where((near[s] == c) & (s < live), s, found)
        inv[c] = found

    xpad[...] = jnp.zeros((bs, bs), f32)
    for c in range(n_blk):
        xpad[0:3, :] = pos_ref[:, c * bs : (c + 1) * bs]
        post[c] = xpad[...].T
    own_t[...] = post[q]

    steps = lax.broadcasted_iota(jnp.int32, (n_m, 2 * n_f), 0).astype(f32) - half_m
    gain = jnp.exp(-0.5 * steps * steps)
    for wd, src in ((wd1, f1_ref), (wd2, f2_ref)):
        wd[...] = jnp.concatenate([src[...], src[...]], axis=1) * gain
    xpad[0:n_m, :] = wd2[...]
    wcol[...] = xpad[...].T

    nf[0:3, :] = wave_ref[...].astype(f32)
    depth_side = n_blk * bs / (atom_density * slab_width * slab_height)
    sides = (slab_width * n_at, slab_height, depth_side)
    scales = [2.0 * math.pi / side for side in sides]
    kx, ky, kz = (nf[a : a + 1, :] * scales[a] for a in range(3))
    square = kx * kx + ky * ky + kz * kz
    weight = jnp.exp(-0.5 * spread_square * square) / (square + screen_square) * (2.0 / total_atoms)
    for c in range(k_chunks):
        wtab[c, 0:1, :] = weight[:, c * bs : (c + 1) * bs]

    rows_t = 16
    span = min(n_wave, 512)

    def tables(block):
        def one(step, carry):
            at = pl.multiple_of(step * rows_t, rows_t)
            cols = []
            for a in range(3):
                col = post[block, pl.ds(at, rows_t), a : a + 1] * (1.0 / sides[a])
                cols.append(col - jnp.round(col))
            row = pl.ds(pl.multiple_of(block * bs + at, rows_t), rows_t)
            for start in range(0, n_wave, span):
                lanes = slice(start, start + span)
                u = cols[0] * nf[0:1, lanes] + cols[1] * nf[1:2, lanes] + cols[2] * nf[2:3, lanes]
                sine, cosine = sin_cos_turns(u - jnp.round(u))
                thi[row, lanes], tlo[row, lanes] = split(cosine)
                later = slice(n_wave + start, n_wave + start + span)
                thi[row, later], tlo[row, later] = split(sine)
            return carry

        lax.fori_loop(0, bs // rows_t, one, 0)

    for block in range(n_blk // 2):
        tables(block)

    rows_g = 32
    centre = cutoff_radius * half_m / (n_m - 1)
    spacing = cutoff_radius / (n_m - 1)
    sharp = 0.5 / spacing ** 2

    def put_values(dest, value, lanes):
        high, low = split(value)
        dest[0:n_f, lanes] = high
        dest[n_f : 2 * n_f, lanes] = low
        dest[2 * n_f : 3 * n_f, lanes] = high
        dest[3 * n_f : 4 * n_f, lanes] = low

    def pairs(s, block):
        lanes = pl.ds(pl.multiple_of(s * bs, bs), bs)
        alive = jnp.where(s < live, 1.0, 0.0).astype(f32)
        put_values(zf, wide[block, 0:n_f, :], lanes)
        right = [wide[block, n_f + a : n_f + a + 1, :] for a in range(3)]
        for start in range(0, bs, rows_g):
            rows = slice(start, start + rows_g)
            dx, dy, dz = (own_t[rows, a : a + 1] - right[a] for a in range(3))
            squared = dx * dx + dy * dy + dz * dz + self_offset
            inverse = lax.rsqrt(squared)
            r = squared * inverse
            i = lax.broadcasted_iota(jnp.int32, (rows_g, bs), 0) + start
            j = lax.broadcasted_iota(jnp.int32, (rows_g, bs), 1)
            off = (i - j) * (i - j) + s
            active = jnp.where((r < cutoff_radius) & (off != 0), alive, 0.0)
            r = jnp.minimum(r, cutoff_radius)
            rho = r - centre
            bell = jnp.exp(-sharp * rho * rho)
            tau = jnp.exp((2.0 * sharp * spacing) * rho)
            tin = jnp.exp((-2.0 * sharp * spacing) * rho)
            sine, cosine = sin_cos_turns(r * (0.25 / cutoff_radius))
            cosine = cosine * active
            cut = cosine * cosine
            slope = (-math.pi / cutoff_radius) * sine * cosine
            first = cut * bell
            geo[0, rows, lanes] = dx
            geo[1, rows, lanes] = dy
            geo[2, rows, lanes] = dz
            geo[3, rows, lanes] = tau
            geo[4, rows, lanes] = tin
            geo[5, rows, lanes] = (slope - (2.0 * sharp) * rho * cut) * bell * inverse
            geo[6, rows, lanes] = (2.0 * sharp * spacing) * first * inverse
            term = first
            for m in range(half_m, n_m):
                out = slice(m * bs + start, m * bs + start + rows_g)
                ahi[out, lanes], alo[out, lanes] = split(term)
                term = term * tau
            term = first
            for m in range(half_m - 1, -1, -1):
                term = term * tin
                out = slice(m * bs + start, m * bs + start + rows_g)
                ahi[out, lanes], alo[out, lanes] = split(term)

    def near_pairs(s, carry):
        pairs(s, near_id(s))
        return carry

    group = 4

    def messages(values, wd, lanes, total):
        stack = values[0 : 2 * n_f, lanes]
        for g in range(0, n_m, group):
            rows = slice(g * bs, (g + group) * bs)
            got = dot_nt(ahi[rows, lanes], stack) + dot_nt(alo[rows, lanes], stack)
            for m in range(group):
                total = total + got[m * bs : (m + 1) * bs] * wd[g + m : g + m + 1, :]
        return total

    def upright(total):
        flipped = total.T
        return flipped[0:n_f] + flipped[n_f:]

    first_lanes, later_lanes = slice(0, bs), slice(bs, wide_n)
    nothing = jnp.zeros((bs, 2 * n_f), f32)
    mine = n_blk + q
    if wide_p > wide_n:
        spare = slice(wide_n, wide_p)
        for values in (zf, zz):
            values[:, spare] = jnp.zeros((4 * n_f, wide_p - wide_n), bf16)
        for index in range(3, 7):
            geo[index, :, spare] = jnp.zeros((bs, wide_p - wide_n), f32)
    pairs(0, mine)
    total = messages(zf, wd1, first_lanes, nothing)
    met(1, rounds[0])
    greet(2, rounds[1])
    wait_bytes(own_rows, halo_r.at[0])
    wait_bytes(own_rows, halo_r.at[1])
    lax.fori_loop(1, n_slot, near_pairs, 0)
    met(2, rounds[1])
    greet(3, rounds[2])
    z_one = wide[mine, 0:n_f, :] + upright(messages(zf, wd1, later_lanes, total))
    zwide[mine] = z_one
    met(0, across)
    for dp, dq in near_peers:
        send(zwide.at[mine], zwide.at[(1 - dp) * n_blk + q], 1, dp, dq)
    for block in range(n_blk // 2, n_blk):
        tables(block)
    met(3, rounds[2])
    greet(4, rounds[3])
    put_values(zz, z_one, first_lanes)
    total = messages(zz, wd2, first_lanes, nothing)
    wait_bytes(zwide.at[pl.ds(0, 3 * n_blk - 1)], rsem.at[1])
    for s in range(1, n_slot):
        put_values(zz, zwide[near[s]], slice(s * bs, (s + 1) * bs))
    z_two = z_one + upright(messages(zz, wd2, later_lanes, total))

    qbuf[q] = exact_nn(cw_ref[...], z_two)
    for dq in range(1, n_k):
        send(qbuf.at[q], qbuf.at[q], 2, 0, dq)
    hidden = exact_tn(rin_ref[...], z_two)
    gate = 1.0 / (1.0 + jnp.exp(-hidden))
    bent = gate * (1.0 + hidden * (1.0 - gate))
    short_grad = exact_nn(rin_ref[...] * rout_ref[...], bent)
    wait_bytes(qbuf.at[pl.ds(0, n_k - 1)], rsem.at[2])

    charges = jnp.concatenate([qbuf[c] for c in range(n_blk)], axis=1)
    stacked = jnp.concatenate(split(charges), axis=0)
    met(4, rounds[3])
    pair_k = n_group // 2
    span_k = pair_k * bs
    groups = n_at // n_group
    own_group, own_place = p // n_group, lax.rem(p, n_group)
    for step in range(groups):
        this = lax.rem(own_group + step, groups)
        for kind in range(2):
            lanes = pl.ds(pl.multiple_of(kind * n_wave + this * span_k, bs), span_k)
            got = dot_nn(stacked, thi[:, lanes]) + dot_nn(stacked, tlo[:, lanes])
            got = got[0:n_q] + got[n_q:]
            for c in range(pair_k):
                sfb[this * n_group + 2 * c + kind] = got[:, c * bs : (c + 1) * bs]
        for c in range(1 if step == 0 else 0, n_group):
            place = lax.rem(own_place + c, n_group)
            target = this * n_group + place
            ahead = lax.rem(target - p + n_at, n_at)
            send(sfb.at[target], rsb.at[ahead - 1], 3, ahead, 0)
    wait_bytes(rsb, rsem.at[3])
    part = sfb[p]
    for d in range(n_at - 1):
        part = part + rsb[d]
    agpart[...] = part * wtab[p // 2, 0:1, :]
    for d in range(1, n_at // 2 + 1):
        for dp in sorted({d, n_at - d}):
            send(agpart, agb.at[p], 4, dp, 0, group_r.at[own_group])
    keep = pltpu.make_async_copy(agpart, agb.at[p], group_r.at[own_group])
    keep.start()

    total = jnp.zeros((n_blk * bs, 8 * n_q), f32)
    for step in range(groups):
        this = lax.rem(own_group + step, groups)
        wait_bytes(agb.at[pl.ds(0, n_group)], group_r.at[this])
        for c in range(pair_k):
            at = pl.multiple_of(this * span_k + c * bs, bs)
            cos_part = agb[this * n_group + 2 * c]
            sin_part = agb[this * n_group + 2 * c + 1]
            ks = [nf[a : a + 1, pl.ds(at, bs)] * scales[a] for a in range(3)]
            rows = [cos_part] + [sin_part * k for k in ks]
            rows2 = [sin_part] + [cos_part * -k for k in ks]
            for kind, pieces in ((0, rows), (1, rows2)):
                place = slice(kind * span_k + c * bs, kind * span_k + (c + 1) * bs)
                for a, piece in enumerate(pieces):
                    high, low = split(piece)
                    rmat[step, a * n_q : (a + 1) * n_q, place] = high
                    rmat[step, (4 + a) * n_q : (5 + a) * n_q, place] = low
        for kind in range(2):
            lanes = pl.ds(pl.multiple_of(kind * n_wave + this * span_k, bs), span_k)
            right = rmat[step, :, kind * span_k : (kind + 1) * span_k]
            total = total + dot_nt(thi[:, lanes], right) + dot_nt(tlo[:, lanes], right)
    got = total
    folded = []
    for c in range(n_blk):
        flipped = got[c * bs : (c + 1) * bs].T
        flipped = flipped[0 : 4 * n_q] + flipped[4 * n_q :]
        cgs[c] = flipped[0:n_q]
        folded.append(flipped)
    for dq in range(1, n_k):
        send(cgs.at[lax.rem(q + dq, n_k)], cgr.at[dq - 1], 5, 0, dq)
    for c in range(n_blk):
        for a in range(3):
            product = qbuf[c] * folded[c][(1 + a) * n_q : (2 + a) * n_q]
            row = a * n_blk + c
            wf[row : row + 1, :] = jnp.sum(product, axis=0, keepdims=True)
    wait_bytes(cgr, rsem.at[5])
    charge_grad = cgs[q] + cgr[0]
    for dq in range(1, n_k - 1):
        charge_grad = charge_grad + cgr[dq]
    g_two = exact_tn(cw_ref[...], charge_grad) + short_grad

    for m in range(n_m):
        lanes = slice(m * bs, (m + 1) * bs)
        high, low = split(g_two * wcol[0:n_f, m : m + 1])
        gwt[0:n_f, lanes] = high
        gwt[n_f:, lanes] = low
    got = dot_nn(gwt[...], ahi[...]) + dot_nn(gwt[...], alo[...])
    got = got[0:n_f] + got[n_f:]
    for s in range(n_slot):
        tslot[s] = got[:, s * bs : (s + 1) * bs]
    tslot[n_slot] = jnp.zeros((n_f, bs), f32)
    for index, (dp, dq) in enumerate(near_peers):
        block = (1 + dp) * n_blk + lax.rem(q + dq, n_k)
        tsend[index] = tslot[inv[block]]
        send(tsend.at[index], trecv.at[index], 6, dp, dq)

    rows_c = 32
    rows_h = 16
    tile = 2 * bs
    tiles = wide_p // tile
    steps_p = bs // rows_c * tiles

    def pair_sums(grad, wd, values, last):
        twice = jnp.concatenate([grad, grad], axis=0).T
        for chunk in range(bs // rows_c):
            for m in range(n_m):
                start = (chunk * n_m + m) * rows_c
                rows = slice(start, start + rows_c)
                high, low = split(twice[chunk * rows_c : (chunk + 1) * rows_c] * wd[m : m + 1, :])
                gw[rows, 0 : 2 * n_f] = high
                gw[rows, 2 * n_f :] = low

        def product(step, buf):
            height = n_m * rows_c
            rows = pl.ds(pl.multiple_of(step // tiles * height, height), height)
            lanes = pl.ds(pl.multiple_of(lax.rem(step, tiles) * tile, tile), tile)
            buf[...] = dot_nn(gw[rows, :], values[:, lanes])

        def horner(step, buf):
            lanes = pl.ds(pl.multiple_of(lax.rem(step, tiles) * tile, tile), tile)
            for part in range(0, rows_c, rows_h):
                rows = pl.ds(pl.multiple_of(step // tiles * rows_c + part, rows_h), rows_h)

                def term(m):
                    return buf[m * rows_c + part : m * rows_c + part + rows_h, :]

                tau = geo[3, rows, lanes]
                tin = geo[4, rows, lanes]
                up = term(n_m - 1)
                up_d = up
                down = term(0)
                down_d = down
                for m in range(1, half_m):
                    down = down * tin + term(m)
                    down_d = down_d * tin + down
                    if m < half_m - 1:
                        up = up * tau + term(n_m - 1 - m)
                        up_d = up_d * tau + up
                up = up * tau + term(half_m)
                zero_sum = up + down * tin
                one_sum = up_d * tau - down_d * tin
                value = geo[5, rows, lanes] * zero_sum + geo[6, rows, lanes] * one_sum
                if last:
                    value = value + qsum[rows, lanes]
                qsum[rows, lanes] = value

        def both(turn, carry):
            step = 2 * turn
            product(step + 1, buf_b)
            horner(step, buf_a)
            product(step + 2, buf_a)
            horner(step + 1, buf_b)
            return carry

        product(0, buf_a)
        lax.fori_loop(0, steps_p // 2 - 1, both, 0)
        product(steps_p - 1, buf_b)
        horner(steps_p - 2, buf_a)
        horner(steps_p - 1, buf_b)

    pair_sums(g_two, wd2, zz, False)
    wait_bytes(trecv, rsem.at[6])
    g_one = g_two + tslot[0]
    for index in range(len(near_peers)):
        g_one = g_one + trecv[index]
    pair_sums(g_one, wd1, zf, True)

    own = [jnp.zeros((bs, bs), f32) for _ in range(3)]
    for s in range(n_slot):
        lanes = slice(s * bs, (s + 1) * bs)
        value = qsum[:, lanes]
        for a in range(3):
            product = value * geo[a, :, lanes]
            own[a] = own[a] + product
            pg[s, a : a + 1, :] = -jnp.sum(product, axis=0, keepdims=True)
    pg[n_slot, 0:3, :] = jnp.zeros((3, bs), f32)
    for a in range(3):
        pg[0, a : a + 1, :] = pg[0, a : a + 1, :] + jnp.sum(own[a].T, axis=0, keepdims=True)
    fsend[...] = jnp.zeros(fsend.shape, f32)
    for side in range(3):
        for c in range(n_blk):
            value = pg[inv[side * n_blk + c], 0:3, :]
            for a in range(3):
                row = a * n_blk + c
                piece = value[a : a + 1]
                if side == 1:
                    piece = piece + wf[row : row + 1, :]
                fsend[side, row : row + 1, :] = piece
    for index, (dp, dq) in enumerate(near_peers):
        send(fsend.at[1 + dp], frecv.at[index], 7, dp, dq)
    wait_bytes(frecv, rsem.at[7])
    force = fsend[1]
    for index in range(len(near_peers)):
        force = force + frecv[index]
    for a in range(3):
        for c in range(n_blk):
            row = a * n_blk + c
            out_ref[a : a + 1, c * bs : (c + 1) * bs] = -force[row : row + 1]

    wait_bytes(wide.at[pl.ds(0, 2 * n_blk)], ssem.at[0])
    wait_bytes(zwide.at[pl.ds(0, 3 * n_blk - 1)], ssem.at[1])
    wait_bytes(qbuf.at[pl.ds(0, n_k - 1)], ssem.at[2])
    wait_bytes(rsb, ssem.at[3])
    wait_bytes(agb.at[pl.ds(0, n_at - 1)], ssem.at[4])
    wait_bytes(cgr, ssem.at[5])
    wait_bytes(trecv, ssem.at[6])
    wait_bytes(frecv, ssem.at[7])


def body(
    n_at, n_k,
    positions, features, filter_one, filter_two, readout_in, readout_out, charge_weight,
    neighbour_blocks, live_slots, wave_ints,
):
    n_f = features.shape[0]
    n_m = filter_one.shape[0]
    n_q = charge_weight.shape[1]
    n_blk, n_slot = neighbour_blocks.shape
    bs = positions.shape[1] // n_blk
    n_wave = wave_ints.shape[1]
    local = n_blk * bs
    wide_n = n_slot * bs
    wide_p = (n_slot + n_slot % 2) * bs
    near_n = 3 * n_blk - 1
    k_chunks = n_wave // bs
    sizes = (n_at, n_k, n_blk, bs, n_slot, n_f, n_m, n_q, n_wave)
    v = pltpu.VMEM
    scratch = [
        v((3 * n_blk, n_f + 8, bs), f32),
        v((3 * n_blk, n_f, bs), f32),
        v((n_blk, bs, bs), f32),
        v((bs, bs), f32),
        v((bs, bs), f32),
        v((8, n_wave), f32),
        v((k_chunks, 8, bs), f32),
        v((local, 2 * n_wave), bf16),
        v((local, 2 * n_wave), bf16),
        v((n_m * bs, wide_n), bf16),
        v((n_m * bs, wide_n), bf16),
        v((4 * n_f, wide_p), bf16),
        v((4 * n_f, wide_p), bf16),
        v((7, bs, wide_p), f32),
        v((n_m, 2 * n_f), f32),
        v((n_m, 2 * n_f), f32),
        v((bs, bs), f32),
        v((2 * n_f, n_m * bs), bf16),
        v((n_m * bs, 4 * n_f), bf16),
        v((n_m * 32, 2 * bs), f32),
        v((n_m * 32, 2 * bs), f32),
        v((bs, wide_p), f32),
        v((n_slot + 1, n_f, bs), f32),
        v((near_n, n_f, bs), f32),
        v((near_n, n_f, bs), f32),
        v((n_k, n_q, bs), f32),
        v((n_at, n_q, bs), f32),
        v((n_at - 1, n_q, bs), f32),
        v((n_at, n_q, bs), f32),
        v((n_q, bs), f32),
        v((n_at // n_group, 8 * n_q, n_group * bs), bf16),
        v((n_blk, n_q, bs), f32),
        v((n_k - 1, n_q, bs), f32),
        v((16, bs), f32),
        v((n_slot + 1, 8, bs), f32),
        v((3, 16, bs), f32),
        v((near_n, 16, bs), f32),
        pltpu.SMEM((3 * n_blk,), jnp.int32),
        pltpu.SemaphoreType.DMA((8,)),
        pltpu.SemaphoreType.DMA((8,)),
        pltpu.SemaphoreType.DMA((2,)),
        pltpu.SemaphoreType.DMA((n_at // n_group,)),
        pltpu.SemaphoreType.REGULAR((5,)),
    ]
    vmem = pl.BlockSpec(memory_space=pltpu.VMEM)
    smem = pl.BlockSpec(memory_space=pltpu.SMEM)
    return pl.pallas_call(
        functools.partial(kernel, sizes),
        out_shape=jax.ShapeDtypeStruct(positions.shape, f32),
        in_specs=[vmem] * 8 + [smem] * 2,
        out_specs=vmem,
        scratch_shapes=scratch,
        compiler_params=pltpu.CompilerParams(
            collective_id=0, has_side_effects=True, vmem_limit_bytes=56 * 2**20
        ),
    )(
        positions, features, filter_one, filter_two, readout_in,
        readout_out.reshape(1, n_f), charge_weight.T, wave_ints, neighbour_blocks, live_slots,
    )


def solution(mesh):
    in_specs = (
        P(None, "atoms"), P(None, "atoms"), P(), P(), P(), P(), P(),
        P("atoms", None), P("atoms"), P(None, "kvec"),
    )
    return jax.shard_map(
        functools.partial(body, mesh.shape["atoms"], mesh.shape["kvec"]),
        mesh=mesh, in_specs=in_specs, out_specs=P(None, "atoms"), check_vma=False,
    )
```

```python
import functools
import math

import jax
import jax.numpy as jnp
import numpy as np
from jax import lax
from jax.experimental import pallas as pl
from jax.experimental.pallas import tpu as pltpu
from jax.sharding import PartitionSpec as P

MESH = pl.DeviceIdType.MESH
highest = lax.Precision.HIGHEST
f32 = jnp.float32
bf16 = jnp.bfloat16
slab_width = 5.0
slab_height = 10.0
atom_density = 0.1
cutoff_radius = 5.0
self_offset = 0.0001
screen_square = 0.25
spread_square = 1.0
n_group = 8


def trig_coefficients():
    u = 0.5 * np.cos(np.pi * (np.arange(4000) + 0.5) / 8000)
    cheb = np.polynomial.chebyshev
    scaled = 8.0 * u * u - 1.0
    out = []
    for values, degree, weight in (
        (np.sin(2 * np.pi * u) / u, 6, u),
        (np.cos(2 * np.pi * u), 6, np.ones_like(u)),
    ):
        fitted = cheb.Chebyshev(cheb.chebfit(scaled, values, degree, w=weight))
        poly = fitted.convert(kind=np.polynomial.Polynomial)
        shifted = poly(np.polynomial.Polynomial([-1.0, 8.0]))
        out.append([float(c) for c in shifted.coef])
    return out


SIN_COEF, COS_COEF = trig_coefficients()


def sin_cos_turns(u):
    square = u * u
    sine = SIN_COEF[-1]
    for c in SIN_COEF[-2::-1]:
        sine = sine * square + c
    cosine = COS_COEF[-1]
    for c in COS_COEF[-2::-1]:
        cosine = cosine * square + c
    return sine * u, cosine


def split(x):
    high = x.astype(bf16)
    return high, (x - high.astype(f32)).astype(bf16)


def dot_nn(a, b):
    return lax.dot_general(a, b, (((1,), (0,)), ((), ())), preferred_element_type=f32)


def exact_nn(a, b):
    return lax.dot_general(
        a, b, (((1,), (0,)), ((), ())), precision=highest, preferred_element_type=f32
    )


def exact_tn(a, b):
    return lax.dot_general(
        a, b, (((0,), (0,)), ((), ())), precision=highest, preferred_element_type=f32
    )


def kernel(
    sizes,
    pos_ref, feat_ref, f1_ref, f2_ref, rin_ref, rout_ref, cw_ref, wave_ref, nb_ref, live_ref,
    out_ref,
    wide, zwide, post, xpad, own_t, nf, wtab, thi, tlo, vhi, vlo, ahi, alo, uhi, ulo, zf, zz, geo,
    wd1, wd2, wcol1, wcol2, gwt, gw, buf_a, buf_b, qsum, tslot, tsend, trecv, qbuf, sfb, rsb, agb, agpart, rmat,
    cgs, cgr, wf, pg, fsend, frecv, inv,
    ssem, rsem, halo_r, group_r, greet_sem,
):
    n_at, n_k, n_blk, bs, n_slot, n_f, n_m, n_q, n_wave = sizes
    total_atoms = n_at * n_blk * bs
    p = lax.axis_index("atoms")
    q = lax.axis_index("kvec")
    half_m = n_m // 2
    wide_n = n_slot * bs
    wide_p = zf.shape[1]
    k_chunks = n_wave // bs
    across = [(0, dq) for dq in range(1, n_k)]
    beside = [(1, 0), (-1, 0)]
    near_peers = [(dp, dq) for dq in range(1, n_k) for dp in (1, -1)] + across + beside

    def peer(dp, dq):
        return {"atoms": lax.rem(p + dp + n_at, n_at), "kvec": lax.rem(q + dq, n_k)}

    def send(src, dst, which, dp, dq, recv=None):
        copy = pltpu.make_async_remote_copy(
            src_ref=src, dst_ref=dst, send_sem=ssem.at[which],
            recv_sem=rsem.at[which] if recv is None else recv,
            device_id=peer(dp, dq), device_id_type=MESH,
        )
        copy.start()

    def wait_bytes(ref, sem):
        pltpu.make_async_copy(ref, ref, sem).wait()

    barrier = pltpu.get_barrier_semaphore()
    partners = across + beside
    for dp, dq in partners:
        pl.semaphore_signal(barrier, inc=1, device_id=peer(dp, dq), device_id_type=MESH)

    def greet(index, group):
        for dp, dq in group:
            pl.semaphore_signal(
                greet_sem.at[index], inc=1, device_id=peer(dp, dq), device_id_type=MESH
            )

    def met(index, group):
        pl.semaphore_wait(greet_sem.at[index], len(group))

    rounds = []
    reach = 1
    while reach < n_at // 2:
        rounds.append([(reach, 0), (-reach, 0)])
        reach *= 2

    for c in range(n_blk):
        lanes = slice(c * bs, (c + 1) * bs)
        wide[n_blk + c, 0:n_f, :] = feat_ref[:, lanes]
        wide[n_blk + c, n_f:, :] = jnp.zeros((8, bs), f32)
        wide[n_blk + c, n_f : n_f + 3, :] = pos_ref[:, lanes]
    pl.semaphore_wait(barrier, len(partners))
    own_rows = wide.at[pl.ds(n_blk, n_blk)]
    send(own_rows, wide.at[pl.ds(0, n_blk)], 0, 1, 0, halo_r.at[0])
    send(own_rows, wide.at[pl.ds(2 * n_blk, n_blk)], 0, -1, 0, halo_r.at[1])
    greet(0, across)
    greet(1, rounds[0])

    live = live_ref[q]
    mine = n_blk + q
    base = (p - 1) * n_blk
    total_blocks = n_at * n_blk

    def near_id(s):
        return jnp.minimum(lax.rem(nb_ref[q, s] - base + total_blocks, total_blocks), 3 * n_blk - 1)

    near = [near_id(s) for s in range(n_slot)]
    for c in range(3 * n_blk):
        found = jnp.int32(n_slot)
        for s in range(n_slot - 1, -1, -1):
            found = jnp.where((near[s] == c) & (s < live), s, found)
        inv[c] = found

    xpad[...] = jnp.zeros((bs, bs), f32)
    for c in range(n_blk):
        xpad[0:3, :] = pos_ref[:, c * bs : (c + 1) * bs]
        post[c] = xpad[...].T
    own_t[...] = post[q]

    steps = lax.broadcasted_iota(jnp.int32, (n_m, 2 * n_f), 0).astype(f32) - half_m
    gain = jnp.exp(-0.5 * steps * steps)
    for wd, src in ((wd1, f1_ref), (wd2, f2_ref)):
        wd[...] = jnp.concatenate([src[...], src[...]], axis=1) * gain
    for wcol, wd in ((wcol1, wd1), (wcol2, wd2)):
        xpad[0:n_m, :] = wd[...]
        wcol[...] = xpad[...].T

    nf[...] = jnp.zeros(nf.shape, f32)
    nf[0:3, :] = wave_ref[...].astype(f32)
    depth_side = n_blk * bs / (atom_density * slab_width * slab_height)
    sides = (slab_width * n_at, slab_height, depth_side)
    scales = [2.0 * math.pi / side for side in sides]
    kx, ky, kz = (nf[a : a + 1, :] * scales[a] for a in range(3))
    square = kx * kx + ky * ky + kz * kz
    weight = jnp.exp(-0.5 * spread_square * square) / (square + screen_square) * (2.0 / total_atoms)
    for c in range(k_chunks):
        wtab[c, 0:1, :] = weight[:, c * bs : (c + 1) * bs]

    rows_t = 16
    span = min(n_wave, 512)

    def tables(block):
        def one(step, carry):
            at = pl.multiple_of(step * rows_t, rows_t)
            cols = []
            for a in range(3):
                col = post[block, pl.ds(at, rows_t), a : a + 1] * (1.0 / sides[a])
                cols.append(col - jnp.round(col))
            row = pl.ds(pl.multiple_of(block * bs + at, rows_t), rows_t)
            for start in range(0, n_wave, span):
                lanes = slice(start, start + span)
                u = cols[0] * nf[0:1, lanes] + cols[1] * nf[1:2, lanes] + cols[2] * nf[2:3, lanes]
                sine, cosine = sin_cos_turns(u - jnp.round(u))
                thi[row, lanes], tlo[row, lanes] = split(cosine)
                later = slice(n_wave + start, n_wave + start + span)
                thi[row, later], tlo[row, later] = split(sine)
            return carry

        lax.fori_loop(0, bs // rows_t, one, 0)

    for block in range(n_blk // 2):
        tables(block)

    rows_g = 32
    centre = cutoff_radius * half_m / (n_m - 1)
    spacing = cutoff_radius / (n_m - 1)
    sharp = 0.5 / spacing ** 2

    def put_values(dest, value, lanes):
        high, low = split(value)
        dest[0:n_f, lanes] = high
        dest[n_f : 2 * n_f, lanes] = low
        dest[2 * n_f : 3 * n_f, lanes] = high
        dest[3 * n_f : 4 * n_f, lanes] = low

    def shape(dx, dy, dz, start, s, alive):
        squared = dx * dx + dy * dy + dz * dz + self_offset
        inverse = lax.rsqrt(squared)
        r = squared * inverse
        i = lax.broadcasted_iota(jnp.int32, (rows_g, bs), 0) + start
        j = lax.broadcasted_iota(jnp.int32, (rows_g, bs), 1)
        off = (i - j) * (i - j) + s
        active = jnp.where((r < cutoff_radius) & (off != 0), alive, 0.0)
        r = jnp.minimum(r, cutoff_radius)
        rho = r - centre
        bell = jnp.exp(-sharp * rho * rho)
        tau = jnp.exp((2.0 * sharp * spacing) * rho)
        tin = jnp.exp((-2.0 * sharp * spacing) * rho)
        sine, cosine = sin_cos_turns(r * (0.25 / cutoff_radius))
        cosine = cosine * active
        return active, inverse, rho, bell, tau, tin, sine, cosine, cosine * cosine

    def upright_pairs(s, block):
        lanes = pl.ds(pl.multiple_of(s * bs, bs), bs)
        alive = jnp.where(s < live, 1.0, 0.0).astype(f32)
        put_values(zf, wide[block, 0:n_f, :], lanes)
        left = wide[block, n_f : n_f + 8, :].T
        right = [wide[mine, n_f + a : n_f + a + 1, :] for a in range(3)]
        for start in range(0, bs, rows_g):
            rows = slice(start, start + rows_g)
            dx, dy, dz = (left[rows, a : a + 1] - right[a] for a in range(3))
            shaped = shape(dx, dy, dz, start, s, alive)
            bell, tau, tin, cut = shaped[3], shaped[4], shaped[5], shaped[8]
            first = cut * bell
            out = pl.ds(pl.multiple_of(s * bs + start, rows_g), rows_g)
            term = first
            for m in range(half_m, n_m):
                place = slice(m * bs, (m + 1) * bs)
                uhi[out, place], ulo[out, place] = split(term)
                term = term * tau
            term = first
            for m in range(half_m - 1, -1, -1):
                term = term * tin
                place = slice(m * bs, (m + 1) * bs)
                uhi[out, place], ulo[out, place] = split(term)

    def near_upright(s, carry):
        upright_pairs(s, near_id(s))
        return carry

    def pairs(s, block):
        lanes = pl.ds(pl.multiple_of(s * bs, bs), bs)
        alive = jnp.where(s < live, 1.0, 0.0).astype(f32)
        right = [wide[block, n_f + a : n_f + a + 1, :] for a in range(3)]
        for start in range(0, bs, rows_g):
            rows = slice(start, start + rows_g)
            dx, dy, dz = (own_t[rows, a : a + 1] - right[a] for a in range(3))
            active, inverse, rho, bell, tau, tin, sine, cosine, cut = shape(dx, dy, dz, start, s, alive)
            slope = (-math.pi / cutoff_radius) * sine * cosine
            first = cut * bell
            geo[0, rows, lanes] = dx
            geo[1, rows, lanes] = dy
            geo[2, rows, lanes] = dz
            geo[3, rows, lanes] = tau
            geo[4, rows, lanes] = tin
            geo[5, rows, lanes] = (slope - (2.0 * sharp) * rho * cut) * bell * inverse
            geo[6, rows, lanes] = (2.0 * sharp * spacing) * first * inverse
            term = first
            for m in range(half_m, n_m):
                out = slice(m * bs + start, m * bs + start + rows_g)
                ahi[out, lanes], alo[out, lanes] = split(term)
                term = term * tau
            term = first
            for m in range(half_m - 1, -1, -1):
                term = term * tin
                out = slice(m * bs + start, m * bs + start + rows_g)
                ahi[out, lanes], alo[out, lanes] = split(term)

    def near_pairs(s, carry):
        pairs(s, near_id(s))
        return carry

    group = 4

    def messages(values, wcol, lanes, total):
        stack = values[0 : 2 * n_f, lanes]
        for g in range(0, n_m, group):
            place = slice(g * bs, (g + group) * bs)
            got = dot_nn(stack, uhi[lanes, place]) + dot_nn(stack, ulo[lanes, place])
            got = got[0:n_f] + got[n_f:]
            for m in range(group):
                weights = wcol[0:n_f, g + m : g + m + 1]
                total = total + got[:, m * bs : (m + 1) * bs] * weights
        return total

    first_lanes, later_lanes = slice(0, bs), slice(bs, wide_n)
    if wide_p > wide_n:
        spare = slice(wide_n, wide_p)
        for values in (zf, zz):
            values[:, spare] = jnp.zeros((4 * n_f, wide_p - wide_n), bf16)
        for index in range(3, 7):
            geo[index, :, spare] = jnp.zeros((bs, wide_p - wide_n), f32)
    upright_pairs(0, mine)
    total = messages(zf, wcol1, first_lanes, wide[mine, 0:n_f, :])
    met(1, rounds[0])
    greet(2, rounds[1])
    wait_bytes(own_rows, halo_r.at[0])
    wait_bytes(own_rows, halo_r.at[1])
    lax.fori_loop(1, n_slot, near_upright, 0)
    met(2, rounds[1])
    greet(3, rounds[2])
    z_one = messages(zf, wcol1, later_lanes, total)
    zwide[mine] = z_one
    met(0, across)
    for dp, dq in near_peers:
        send(zwide.at[mine], zwide.at[(1 - dp) * n_blk + q], 1, dp, dq)
    for block in range(n_blk // 2, n_blk):
        tables(block)
    met(3, rounds[2])
    greet(4, rounds[3])
    put_values(zz, z_one, first_lanes)
    total = messages(zz, wcol2, first_lanes, z_one)
    wait_bytes(zwide.at[pl.ds(0, 3 * n_blk - 1)], rsem.at[1])
    for s in range(1, n_slot):
        put_values(zz, zwide[near[s]], slice(s * bs, (s + 1) * bs))
    z_two = messages(zz, wcol2, later_lanes, total)

    qbuf[q] = exact_nn(cw_ref[...], z_two)
    for dq in range(1, n_k):
        send(qbuf.at[q], qbuf.at[q], 2, 0, dq)
    hidden = exact_tn(rin_ref[...], z_two)
    gate = 1.0 / (1.0 + jnp.exp(-hidden))
    bent = gate * (1.0 + hidden * (1.0 - gate))
    short_grad = exact_nn(rin_ref[...] * rout_ref[...], bent)
    wait_bytes(qbuf.at[pl.ds(0, n_k - 1)], rsem.at[2])

    charges = jnp.concatenate([qbuf[c] for c in range(n_blk)], axis=1)
    stacked = jnp.concatenate(split(charges), axis=0)
    met(4, rounds[3])
    pair_k = n_group // 2
    span_k = pair_k * bs
    groups = n_at // n_group
    own_group, own_place = p // n_group, lax.rem(p, n_group)
    for step in range(groups):
        this = lax.rem(own_group + step, groups)
        for kind in range(2):
            lanes = pl.ds(pl.multiple_of(kind * n_wave + this * span_k, bs), span_k)
            got = dot_nn(stacked, thi[:, lanes]) + dot_nn(stacked, tlo[:, lanes])
            got = got[0:n_q] + got[n_q:]
            for c in range(pair_k):
                sfb[this * n_group + 2 * c + kind] = got[:, c * bs : (c + 1) * bs]
        for c in range(1 if step == 0 else 0, n_group):
            place = lax.rem(own_place + c, n_group)
            target = this * n_group + place
            ahead = lax.rem(target - p + n_at, n_at)
            send(sfb.at[target], rsb.at[ahead - 1], 3, ahead, 0)
    pairs(0, mine)
    lax.fori_loop(1, n_slot, near_pairs, 0)
    wait_bytes(rsb, rsem.at[3])
    part = sfb[p]
    for d in range(n_at - 1):
        part = part + rsb[d]
    agpart[...] = part * wtab[p // 2, 0:1, :]
    for d in range(1, n_at // 2 + 1):
        for dp in sorted({d, n_at - d}):
            send(agpart, agb.at[p], 4, dp, 0, group_r.at[own_group])
    keep = pltpu.make_async_copy(agpart, agb.at[p], group_r.at[own_group])
    keep.start()

    places = []
    for a in range(3):
        turns = pos_ref[a : a + 1, :] * (1.0 / sides[a])
        places.append(turns - jnp.round(turns))

    def upright_tables(chunk, carry):
        at = pl.multiple_of(chunk * bs, bs)
        down = nf[:, pl.ds(at, bs)].T
        for start in range(0, bs, rows_t):
            ks = [down[start : start + rows_t, a : a + 1] for a in range(3)]
            u = ks[0] * places[0] + ks[1] * places[1] + ks[2] * places[2]
            sine, cosine = sin_cos_turns(u - jnp.round(u))
            row = pl.ds(pl.multiple_of(at + start, rows_t), rows_t)
            vhi[row, :], vlo[row, :] = split(cosine)
            row = pl.ds(pl.multiple_of(n_wave + at + start, rows_t), rows_t)
            vhi[row, :], vlo[row, :] = split(sine)
        return carry

    lax.fori_loop(0, k_chunks, upright_tables, 0)

    total = jnp.zeros((8 * n_q, n_blk * bs), f32)
    for step in range(groups):
        this = lax.rem(own_group + step, groups)
        wait_bytes(agb.at[pl.ds(0, n_group)], group_r.at[this])
        for c in range(pair_k):
            at = pl.multiple_of(this * span_k + c * bs, bs)
            cos_part = agb[this * n_group + 2 * c]
            sin_part = agb[this * n_group + 2 * c + 1]
            ks = [nf[a : a + 1, pl.ds(at, bs)] * scales[a] for a in range(3)]
            rows = [cos_part] + [sin_part * k for k in ks]
            rows2 = [sin_part] + [cos_part * -k for k in ks]
            for kind, pieces in ((0, rows), (1, rows2)):
                place = slice(kind * span_k + c * bs, kind * span_k + (c + 1) * bs)
                for a, piece in enumerate(pieces):
                    high, low = split(piece)
                    rmat[step, a * n_q : (a + 1) * n_q, place] = high
                    rmat[step, (4 + a) * n_q : (5 + a) * n_q, place] = low
        for kind in range(2):
            lanes = pl.ds(pl.multiple_of(kind * n_wave + this * span_k, bs), span_k)
            right = rmat[step, :, kind * span_k : (kind + 1) * span_k]
            total = total + dot_nn(right, vhi[lanes, :]) + dot_nn(right, vlo[lanes, :])
    total = total[0 : 4 * n_q] + total[4 * n_q :]
    folded = []
    for c in range(n_blk):
        folded.append(total[:, c * bs : (c + 1) * bs])
        cgs[c] = folded[c][0:n_q]
    for dq in range(1, n_k):
        send(cgs.at[lax.rem(q + dq, n_k)], cgr.at[dq - 1], 5, 0, dq)
    for c in range(n_blk):
        for a in range(3):
            product = qbuf[c] * folded[c][(1 + a) * n_q : (2 + a) * n_q]
            row = a * n_blk + c
            wf[row : row + 1, :] = jnp.sum(product, axis=0, keepdims=True)
    wait_bytes(cgr, rsem.at[5])
    charge_grad = cgs[q] + cgr[0]
    for dq in range(1, n_k - 1):
        charge_grad = charge_grad + cgr[dq]
    g_two = exact_tn(cw_ref[...], charge_grad) + short_grad

    for m in range(n_m):
        lanes = slice(m * bs, (m + 1) * bs)
        high, low = split(g_two * wcol2[0:n_f, m : m + 1])
        gwt[0:n_f, lanes] = high
        gwt[n_f:, lanes] = low
    got = dot_nn(gwt[...], ahi[...]) + dot_nn(gwt[...], alo[...])
    got = got[0:n_f] + got[n_f:]
    for s in range(n_slot):
        tslot[s] = got[:, s * bs : (s + 1) * bs]
    tslot[n_slot] = jnp.zeros((n_f, bs), f32)
    for index, (dp, dq) in enumerate(near_peers):
        block = (1 + dp) * n_blk + lax.rem(q + dq, n_k)
        tsend[index] = tslot[inv[block]]
        send(tsend.at[index], trecv.at[index], 6, dp, dq)

    rows_c = 32
    rows_h = 16
    tile = 2 * bs
    tiles = wide_p // tile
    steps_p = bs // rows_c * tiles

    def pair_sums(grad, wd, values, last):
        twice = jnp.concatenate([grad, grad], axis=0).T
        for chunk in range(bs // rows_c):
            for m in range(n_m):
                start = (chunk * n_m + m) * rows_c
                rows = slice(start, start + rows_c)
                high, low = split(twice[chunk * rows_c : (chunk + 1) * rows_c] * wd[m : m + 1, :])
                gw[rows, 0 : 2 * n_f] = high
                gw[rows, 2 * n_f :] = low

        def product(step, buf):
            height = n_m * rows_c
            rows = pl.ds(pl.multiple_of(step // tiles * height, height), height)
            lanes = pl.ds(pl.multiple_of(lax.rem(step, tiles) * tile, tile), tile)
            buf[...] = dot_nn(gw[rows, :], values[:, lanes])

        def horner(step, buf):
            lanes = pl.ds(pl.multiple_of(lax.rem(step, tiles) * tile, tile), tile)
            for part in range(0, rows_c, rows_h):
                rows = pl.ds(pl.multiple_of(step // tiles * rows_c + part, rows_h), rows_h)

                def term(m):
                    return buf[m * rows_c + part : m * rows_c + part + rows_h, :]

                tau = geo[3, rows, lanes]
                tin = geo[4, rows, lanes]
                up = term(n_m - 1)
                up_d = up
                down = term(0)
                down_d = down
                for m in range(1, half_m):
                    down = down * tin + term(m)
                    down_d = down_d * tin + down
                    if m < half_m - 1:
                        up = up * tau + term(n_m - 1 - m)
                        up_d = up_d * tau + up
                up = up * tau + term(half_m)
                zero_sum = up + down * tin
                one_sum = up_d * tau - down_d * tin
                value = geo[5, rows, lanes] * zero_sum + geo[6, rows, lanes] * one_sum
                if last:
                    value = value + qsum[rows, lanes]
                qsum[rows, lanes] = value

        def both(turn, carry):
            step = 2 * turn
            product(step + 1, buf_b)
            horner(step, buf_a)
            product(step + 2, buf_a)
            horner(step + 1, buf_b)
            return carry

        product(0, buf_a)
        lax.fori_loop(0, steps_p // 2 - 1, both, 0)
        product(steps_p - 1, buf_b)
        horner(steps_p - 2, buf_a)
        horner(steps_p - 1, buf_b)

    pair_sums(g_two, wd2, zz, False)
    wait_bytes(trecv, rsem.at[6])
    g_one = g_two + tslot[0]
    for index in range(len(near_peers)):
        g_one = g_one + trecv[index]
    pair_sums(g_one, wd1, zf, True)

    own = [jnp.zeros((bs, bs), f32) for _ in range(3)]
    for s in range(n_slot):
        lanes = slice(s * bs, (s + 1) * bs)
        value = qsum[:, lanes]
        for a in range(3):
            product = value * geo[a, :, lanes]
            own[a] = own[a] + product
            pg[s, a : a + 1, :] = -jnp.sum(product, axis=0, keepdims=True)
    pg[n_slot, 0:3, :] = jnp.zeros((3, bs), f32)
    for a in range(3):
        pg[0, a : a + 1, :] = pg[0, a : a + 1, :] + jnp.sum(own[a].T, axis=0, keepdims=True)
    fsend[...] = jnp.zeros(fsend.shape, f32)
    for side in range(3):
        for c in range(n_blk):
            value = pg[inv[side * n_blk + c], 0:3, :]
            for a in range(3):
                row = a * n_blk + c
                piece = value[a : a + 1]
                if side == 1:
                    piece = piece + wf[row : row + 1, :]
                fsend[side, row : row + 1, :] = piece
    for index, (dp, dq) in enumerate(near_peers):
        send(fsend.at[1 + dp], frecv.at[index], 7, dp, dq)
    wait_bytes(frecv, rsem.at[7])
    force = fsend[1]
    for index in range(len(near_peers)):
        force = force + frecv[index]
    for a in range(3):
        for c in range(n_blk):
            row = a * n_blk + c
            out_ref[a : a + 1, c * bs : (c + 1) * bs] = -force[row : row + 1]

    wait_bytes(wide.at[pl.ds(0, 2 * n_blk)], ssem.at[0])
    wait_bytes(zwide.at[pl.ds(0, 3 * n_blk - 1)], ssem.at[1])
    wait_bytes(qbuf.at[pl.ds(0, n_k - 1)], ssem.at[2])
    wait_bytes(rsb, ssem.at[3])
    wait_bytes(agb.at[pl.ds(0, n_at - 1)], ssem.at[4])
    wait_bytes(cgr, ssem.at[5])
    wait_bytes(trecv, ssem.at[6])
    wait_bytes(frecv, ssem.at[7])


def body(
    n_at, n_k,
    positions, features, filter_one, filter_two, readout_in, readout_out, charge_weight,
    neighbour_blocks, live_slots, wave_ints,
):
    n_f = features.shape[0]
    n_m = filter_one.shape[0]
    n_q = charge_weight.shape[1]
    n_blk, n_slot = neighbour_blocks.shape
    bs = positions.shape[1] // n_blk
    n_wave = wave_ints.shape[1]
    local = n_blk * bs
    wide_n = n_slot * bs
    wide_p = (n_slot + n_slot % 2) * bs
    near_n = 3 * n_blk - 1
    k_chunks = n_wave // bs
    sizes = (n_at, n_k, n_blk, bs, n_slot, n_f, n_m, n_q, n_wave)
    v = pltpu.VMEM
    scratch = [
        v((3 * n_blk, n_f + 8, bs), f32),
        v((3 * n_blk, n_f, bs), f32),
        v((n_blk, bs, bs), f32),
        v((bs, bs), f32),
        v((bs, bs), f32),
        v((8, n_wave), f32),
        v((k_chunks, 8, bs), f32),
        v((local, 2 * n_wave), bf16),
        v((local, 2 * n_wave), bf16),
        v((2 * n_wave, local), bf16),
        v((2 * n_wave, local), bf16),
        v((n_m * bs, wide_n), bf16),
        v((n_m * bs, wide_n), bf16),
        v((wide_n, n_m * bs), bf16),
        v((wide_n, n_m * bs), bf16),
        v((4 * n_f, wide_p), bf16),
        v((4 * n_f, wide_p), bf16),
        v((7, bs, wide_p), f32),
        v((n_m, 2 * n_f), f32),
        v((n_m, 2 * n_f), f32),
        v((bs, bs), f32),
        v((bs, bs), f32),
        v((2 * n_f, n_m * bs), bf16),
        v((n_m * bs, 4 * n_f), bf16),
        v((n_m * 32, 2 * bs), f32),
        v((n_m * 32, 2 * bs), f32),
        v((bs, wide_p), f32),
        v((n_slot + 1, n_f, bs), f32),
        v((near_n, n_f, bs), f32),
        v((near_n, n_f, bs), f32),
        v((n_k, n_q, bs), f32),
        v((n_at, n_q, bs), f32),
        v((n_at - 1, n_q, bs), f32),
        v((n_at, n_q, bs), f32),
        v((n_q, bs), f32),
        v((n_at // n_group, 8 * n_q, n_group * bs), bf16),
        v((n_blk, n_q, bs), f32),
        v((n_k - 1, n_q, bs), f32),
        v((16, bs), f32),
        v((n_slot + 1, 8, bs), f32),
        v((3, 16, bs), f32),
        v((near_n, 16, bs), f32),
        pltpu.SMEM((3 * n_blk,), jnp.int32),
        pltpu.SemaphoreType.DMA((8,)),
        pltpu.SemaphoreType.DMA((8,)),
        pltpu.SemaphoreType.DMA((2,)),
        pltpu.SemaphoreType.DMA((n_at // n_group,)),
        pltpu.SemaphoreType.REGULAR((5,)),
    ]
    vmem = pl.BlockSpec(memory_space=pltpu.VMEM)
    smem = pl.BlockSpec(memory_space=pltpu.SMEM)
    return pl.pallas_call(
        functools.partial(kernel, sizes),
        out_shape=jax.ShapeDtypeStruct(positions.shape, f32),
        in_specs=[vmem] * 8 + [smem] * 2,
        out_specs=vmem,
        scratch_shapes=scratch,
        compiler_params=pltpu.CompilerParams(
            collective_id=0, has_side_effects=True, vmem_limit_bytes=56 * 2**20
        ),
    )(
        positions, features, filter_one, filter_two, readout_in,
        readout_out.reshape(1, n_f), charge_weight.T, wave_ints, neighbour_blocks, live_slots,
    )


def solution(mesh):
    in_specs = (
        P(None, "atoms"), P(None, "atoms"), P(), P(), P(), P(), P(),
        P("atoms", None), P("atoms"), P(None, "kvec"),
    )
    return jax.shard_map(
        functools.partial(body, mesh.shape["atoms"], mesh.shape["kvec"]),
        mesh=mesh, in_specs=in_specs, out_specs=P(None, "atoms"), check_vma=False,
    )
```

```python
import functools
import math

import jax
import jax.numpy as jnp
import numpy as np
from jax import lax
from jax.experimental import pallas as pl
from jax.experimental.pallas import tpu as pltpu
from jax.sharding import PartitionSpec as P

MESH = pl.DeviceIdType.MESH
highest = lax.Precision.HIGHEST
f32 = jnp.float32
bf16 = jnp.bfloat16
slab_width = 5.0
slab_height = 10.0
atom_density = 0.1
cutoff_radius = 5.0
self_offset = 0.0001
screen_square = 0.25
spread_square = 1.0
n_group = 8


def trig_coefficients():
    u = 0.5 * np.cos(np.pi * (np.arange(4000) + 0.5) / 8000)
    cheb = np.polynomial.chebyshev
    scaled = 8.0 * u * u - 1.0
    out = []
    for values, degree, weight in (
        (np.sin(2 * np.pi * u) / u, 6, u),
        (np.cos(2 * np.pi * u), 6, np.ones_like(u)),
    ):
        fitted = cheb.Chebyshev(cheb.chebfit(scaled, values, degree, w=weight))
        poly = fitted.convert(kind=np.polynomial.Polynomial)
        shifted = poly(np.polynomial.Polynomial([-1.0, 8.0]))
        out.append([float(c) for c in shifted.coef])
    return out


SIN_COEF, COS_COEF = trig_coefficients()


def sin_cos_turns(u):
    square = u * u
    sine = SIN_COEF[-1]
    for c in SIN_COEF[-2::-1]:
        sine = sine * square + c
    cosine = COS_COEF[-1]
    for c in COS_COEF[-2::-1]:
        cosine = cosine * square + c
    return sine * u, cosine


def split(x):
    high = x.astype(bf16)
    return high, (x - high.astype(f32)).astype(bf16)


def dot_nn(a, b):
    return lax.dot_general(a, b, (((1,), (0,)), ((), ())), preferred_element_type=f32)


def exact_nn(a, b):
    return lax.dot_general(
        a, b, (((1,), (0,)), ((), ())), precision=highest, preferred_element_type=f32
    )


def exact_tn(a, b):
    return lax.dot_general(
        a, b, (((0,), (0,)), ((), ())), precision=highest, preferred_element_type=f32
    )


def kernel(
    sizes,
    pos_ref, feat_ref, f1_ref, f2_ref, rin_ref, rout_ref, cw_ref, wave_ref, nb_ref, live_ref,
    out_ref,
    wide, zwide, post, xpad, own_t, nf, wtab, tab, vmat, amat, umat, zf, zz, geo,
    wd1, wd2, wcol1, wcol2, gwt, gw, buf_a, buf_b, qsum, tslot, tsend, trecv, qbuf, sfb, rsb, agb, agpart, rmat,
    cgs, cgr, wf, pg, fsend, frecv, inv,
    ssem, rsem, halo_r, group_r, greet_sem,
):
    n_at, n_k, n_blk, bs, n_slot, n_f, n_m, n_q, n_wave = sizes
    total_atoms = n_at * n_blk * bs
    p = lax.axis_index("atoms")
    q = lax.axis_index("kvec")
    half_m = n_m // 2
    wide_n = n_slot * bs
    wide_p = zf.shape[1]
    k_chunks = n_wave // bs
    across = [(0, dq) for dq in range(1, n_k)]
    beside = [(1, 0), (-1, 0)]
    near_peers = [(dp, dq) for dq in range(1, n_k) for dp in (1, -1)] + across + beside

    def peer(dp, dq):
        return {"atoms": lax.rem(p + dp + n_at, n_at), "kvec": lax.rem(q + dq, n_k)}

    def send(src, dst, which, dp, dq, recv=None):
        copy = pltpu.make_async_remote_copy(
            src_ref=src, dst_ref=dst, send_sem=ssem.at[which],
            recv_sem=rsem.at[which] if recv is None else recv,
            device_id=peer(dp, dq), device_id_type=MESH,
        )
        copy.start()

    def wait_bytes(ref, sem):
        pltpu.make_async_copy(ref, ref, sem).wait()

    barrier = pltpu.get_barrier_semaphore()
    partners = across + beside
    for dp, dq in partners:
        pl.semaphore_signal(barrier, inc=1, device_id=peer(dp, dq), device_id_type=MESH)

    def greet(index, group):
        for dp, dq in group:
            pl.semaphore_signal(
                greet_sem.at[index], inc=1, device_id=peer(dp, dq), device_id_type=MESH
            )

    def met(index, group):
        pl.semaphore_wait(greet_sem.at[index], len(group))

    rounds = []
    reach = 1
    while reach < n_at // 2:
        rounds.append([(reach, 0), (-reach, 0)])
        reach *= 2

    for c in range(n_blk):
        lanes = slice(c * bs, (c + 1) * bs)
        wide[n_blk + c, 0:n_f, :] = feat_ref[:, lanes]
        wide[n_blk + c, n_f:, :] = jnp.zeros((8, bs), f32)
        wide[n_blk + c, n_f : n_f + 3, :] = pos_ref[:, lanes]
    pl.semaphore_wait(barrier, len(partners))
    own_rows = wide.at[pl.ds(n_blk, n_blk)]
    send(own_rows, wide.at[pl.ds(0, n_blk)], 0, 1, 0, halo_r.at[0])
    send(own_rows, wide.at[pl.ds(2 * n_blk, n_blk)], 0, -1, 0, halo_r.at[1])
    greet(0, across)
    greet(1, rounds[0])

    live = live_ref[q]
    mine = n_blk + q
    base = (p - 1) * n_blk
    total_blocks = n_at * n_blk

    def near_id(s):
        return jnp.minimum(lax.rem(nb_ref[q, s] - base + total_blocks, total_blocks), 3 * n_blk - 1)

    near = [near_id(s) for s in range(n_slot)]
    for c in range(3 * n_blk):
        found = jnp.int32(n_slot)
        for s in range(n_slot - 1, -1, -1):
            found = jnp.where((near[s] == c) & (s < live), s, found)
        inv[c] = found

    xpad[...] = jnp.zeros((bs, bs), f32)
    for c in range(n_blk):
        xpad[0:3, :] = pos_ref[:, c * bs : (c + 1) * bs]
        post[c] = xpad[...].T
    own_t[...] = post[q]

    steps = lax.broadcasted_iota(jnp.int32, (n_m, 2 * n_f), 0).astype(f32) - half_m
    gain = jnp.exp(-0.5 * steps * steps)
    for wd, src in ((wd1, f1_ref), (wd2, f2_ref)):
        wd[...] = jnp.concatenate([src[...], src[...]], axis=1) * gain
    for wcol, wd in ((wcol1, wd1), (wcol2, wd2)):
        xpad[0:n_m, :] = wd[...]
        wcol[...] = xpad[...].T

    nf[...] = jnp.zeros(nf.shape, f32)
    nf[0:3, :] = wave_ref[...].astype(f32)
    depth_side = n_blk * bs / (atom_density * slab_width * slab_height)
    sides = (slab_width * n_at, slab_height, depth_side)
    scales = [2.0 * math.pi / side for side in sides]
    kx, ky, kz = (nf[a : a + 1, :] * scales[a] for a in range(3))
    square = kx * kx + ky * ky + kz * kz
    weight = jnp.exp(-0.5 * spread_square * square) / (square + screen_square) * (2.0 / total_atoms)
    for c in range(k_chunks):
        wtab[c, 0:1, :] = weight[:, c * bs : (c + 1) * bs]

    rows_t = 16
    span = min(n_wave, 512)

    def tables(block):
        def one(step, carry):
            at = pl.multiple_of(step * rows_t, rows_t)
            cols = []
            for a in range(3):
                col = post[block, pl.ds(at, rows_t), a : a + 1] * (1.0 / sides[a])
                cols.append(col - jnp.round(col))
            row = pl.ds(pl.multiple_of(block * bs + at, rows_t), rows_t)
            low_row = pl.ds(pl.multiple_of((n_blk + block) * bs + at, rows_t), rows_t)
            for start in range(0, n_wave, span):
                lanes = slice(start, start + span)
                u = cols[0] * nf[0:1, lanes] + cols[1] * nf[1:2, lanes] + cols[2] * nf[2:3, lanes]
                sine, cosine = sin_cos_turns(u - jnp.round(u))
                tab[row, lanes], tab[low_row, lanes] = split(cosine)
                later = slice(n_wave + start, n_wave + start + span)
                tab[row, later], tab[low_row, later] = split(sine)
            return carry

        lax.fori_loop(0, bs // rows_t, one, 0)

    for block in range(n_blk // 2):
        tables(block)

    rows_g = 32
    centre = cutoff_radius * half_m / (n_m - 1)
    spacing = cutoff_radius / (n_m - 1)
    sharp = 0.5 / spacing ** 2

    def put_values(dest, value, lanes):
        high, low = split(value)
        dest[0:n_f, lanes] = high
        dest[n_f : 2 * n_f, lanes] = low
        dest[2 * n_f : 3 * n_f, lanes] = high
        dest[3 * n_f : 4 * n_f, lanes] = low

    def shape(dx, dy, dz, start, s, alive):
        squared = dx * dx + dy * dy + dz * dz + self_offset
        inverse = lax.rsqrt(squared)
        r = squared * inverse
        i = lax.broadcasted_iota(jnp.int32, (rows_g, bs), 0) + start
        j = lax.broadcasted_iota(jnp.int32, (rows_g, bs), 1)
        off = (i - j) * (i - j) + s
        active = jnp.where((r < cutoff_radius) & (off != 0), alive, 0.0)
        r = jnp.minimum(r, cutoff_radius)
        rho = r - centre
        bell = jnp.exp(-sharp * rho * rho)
        tau = jnp.exp((2.0 * sharp * spacing) * rho)
        tin = jnp.exp((-2.0 * sharp * spacing) * rho)
        sine, cosine = sin_cos_turns(r * (0.25 / cutoff_radius))
        cosine = cosine * active
        return active, inverse, rho, bell, tau, tin, sine, cosine, cosine * cosine

    def upright_pairs(s, block, high_at, low_at):
        lanes = pl.ds(pl.multiple_of(s * bs, bs), bs)
        alive = jnp.where(s < live, 1.0, 0.0).astype(f32)
        put_values(zf, wide[block, 0:n_f, :], lanes)
        left = wide[block, n_f : n_f + 8, :].T
        right = [wide[mine, n_f + a : n_f + a + 1, :] for a in range(3)]
        for start in range(0, bs, rows_g):
            rows = slice(start, start + rows_g)
            dx, dy, dz = (left[rows, a : a + 1] - right[a] for a in range(3))
            shaped = shape(dx, dy, dz, start, s, alive)
            bell, tau, tin, cut = shaped[3], shaped[4], shaped[5], shaped[8]
            first = cut * bell
            out = pl.ds(pl.multiple_of(high_at + start, rows_g), rows_g)
            low_out = pl.ds(pl.multiple_of(low_at + start, rows_g), rows_g)
            term = first
            for m in range(half_m, n_m):
                place = slice(m * bs, (m + 1) * bs)
                umat[out, place], umat[low_out, place] = split(term)
                term = term * tau
            term = first
            for m in range(half_m - 1, -1, -1):
                term = term * tin
                place = slice(m * bs, (m + 1) * bs)
                umat[out, place], umat[low_out, place] = split(term)

    def near_upright(s, carry):
        upright_pairs(s, near_id(s), (s + 1) * bs, (s + n_slot) * bs)
        return carry

    def pairs(s, block):
        lanes = pl.ds(pl.multiple_of(s * bs, bs), bs)
        alive = jnp.where(s < live, 1.0, 0.0).astype(f32)
        right = [wide[block, n_f + a : n_f + a + 1, :] for a in range(3)]
        for start in range(0, bs, rows_g):
            rows = slice(start, start + rows_g)
            dx, dy, dz = (own_t[rows, a : a + 1] - right[a] for a in range(3))
            active, inverse, rho, bell, tau, tin, sine, cosine, cut = shape(dx, dy, dz, start, s, alive)
            slope = (-math.pi / cutoff_radius) * sine * cosine
            first = cut * bell
            geo[0, rows, lanes] = dx
            geo[1, rows, lanes] = dy
            geo[2, rows, lanes] = dz
            geo[3, rows, lanes] = tau
            geo[4, rows, lanes] = tin
            geo[5, rows, lanes] = (slope - (2.0 * sharp) * rho * cut) * bell * inverse
            geo[6, rows, lanes] = (2.0 * sharp * spacing) * first * inverse
            term = first
            for m in range(half_m, n_m):
                out = slice(m * bs + start, m * bs + start + rows_g)
                low_out = slice(out.start + n_m * bs, out.stop + n_m * bs)
                amat[out, lanes], amat[low_out, lanes] = split(term)
                term = term * tau
            term = first
            for m in range(half_m - 1, -1, -1):
                term = term * tin
                out = slice(m * bs + start, m * bs + start + rows_g)
                low_out = slice(out.start + n_m * bs, out.stop + n_m * bs)
                amat[out, lanes], amat[low_out, lanes] = split(term)

    def near_pairs(s, carry):
        pairs(s, near_id(s))
        return carry

    group = 4

    def messages(values, wcol, lanes, total):
        stack = values[0 : 2 * n_f, lanes]
        stack = jnp.concatenate([stack, stack], axis=1)
        for g in range(0, n_m, group):
            place = slice(g * bs, (g + group) * bs)
            got = dot_nn(stack, umat[2 * lanes.start : 2 * lanes.stop, place])
            got = got[0:n_f] + got[n_f:]
            for m in range(group):
                weights = wcol[0:n_f, g + m : g + m + 1]
                total = total + got[:, m * bs : (m + 1) * bs] * weights
        return total

    first_lanes, later_lanes = slice(0, bs), slice(bs, wide_n)
    if wide_p > wide_n:
        spare = slice(wide_n, wide_p)
        for values in (zf, zz):
            values[:, spare] = jnp.zeros((4 * n_f, wide_p - wide_n), bf16)
        for index in range(3, 7):
            geo[index, :, spare] = jnp.zeros((bs, wide_p - wide_n), f32)
    upright_pairs(0, mine, 0, bs)
    total = messages(zf, wcol1, first_lanes, wide[mine, 0:n_f, :])
    met(1, rounds[0])
    greet(2, rounds[1])
    wait_bytes(own_rows, halo_r.at[0])
    wait_bytes(own_rows, halo_r.at[1])
    lax.fori_loop(1, n_slot, near_upright, 0)
    met(2, rounds[1])
    greet(3, rounds[2])
    z_one = messages(zf, wcol1, later_lanes, total)
    zwide[mine] = z_one
    met(0, across)
    for dp, dq in near_peers:
        send(zwide.at[mine], zwide.at[(1 - dp) * n_blk + q], 1, dp, dq)
    for block in range(n_blk // 2, n_blk):
        tables(block)
    met(3, rounds[2])
    greet(4, rounds[3])
    put_values(zz, z_one, first_lanes)
    total = messages(zz, wcol2, first_lanes, z_one)
    wait_bytes(zwide.at[pl.ds(0, 3 * n_blk - 1)], rsem.at[1])
    for s in range(1, n_slot):
        put_values(zz, zwide[near[s]], slice(s * bs, (s + 1) * bs))
    z_two = messages(zz, wcol2, later_lanes, total)

    qbuf[q] = exact_nn(cw_ref[...], z_two)
    for dq in range(1, n_k):
        send(qbuf.at[q], qbuf.at[q], 2, 0, dq)
    hidden = exact_tn(rin_ref[...], z_two)
    gate = 1.0 / (1.0 + jnp.exp(-hidden))
    bent = gate * (1.0 + hidden * (1.0 - gate))
    short_grad = exact_nn(rin_ref[...] * rout_ref[...], bent)

    pair_k = n_group // 2
    span_k = pair_k * bs
    groups = n_at // n_group
    places = []
    for a in range(3):
        turns = pos_ref[a : a + 1, :] * (1.0 / sides[a])
        places.append(turns - jnp.round(turns))

    def upright_tables(chunk, carry):
        down = nf[:, pl.ds(pl.multiple_of(chunk * bs, bs), bs)].T
        at = (chunk // pair_k) * (4 * span_k) + lax.rem(chunk, pair_k) * bs
        for start in range(0, bs, rows_t):
            ks = [down[start : start + rows_t, a : a + 1] for a in range(3)]
            u = ks[0] * places[0] + ks[1] * places[1] + ks[2] * places[2]
            sine, cosine = sin_cos_turns(u - jnp.round(u))
            rows = [
                pl.ds(pl.multiple_of(at + part * span_k + start, rows_t), rows_t)
                for part in range(4)
            ]
            vmat[rows[0], :], vmat[rows[2], :] = split(cosine)
            vmat[rows[1], :], vmat[rows[3], :] = split(sine)
        return carry

    q_chunks, rs_chunks = k_chunks * 7 // 16, k_chunks * 10 // 16
    lax.fori_loop(0, q_chunks, upright_tables, 0)
    wait_bytes(qbuf.at[pl.ds(0, n_k - 1)], rsem.at[2])

    charges = jnp.concatenate([qbuf[c] for c in range(n_blk)], axis=1)
    stacked = jnp.concatenate(split(charges), axis=0)
    stacked = jnp.concatenate([stacked, stacked], axis=1)
    met(4, rounds[3])
    own_group, own_place = p // n_group, lax.rem(p, n_group)
    for step in range(groups):
        this = lax.rem(own_group + step, groups)
        for kind in range(2):
            lanes = pl.ds(pl.multiple_of(kind * n_wave + this * span_k, bs), span_k)
            got = dot_nn(stacked, tab[:, lanes])
            got = got[0:n_q] + got[n_q:]
            for c in range(pair_k):
                sfb[this * n_group + 2 * c + kind] = got[:, c * bs : (c + 1) * bs]
        for c in range(1 if step == 0 else 0, n_group):
            place = lax.rem(own_place + c, n_group)
            target = this * n_group + place
            ahead = lax.rem(target - p + n_at, n_at)
            send(sfb.at[target], rsb.at[ahead - 1], 3, ahead, 0)
    pairs(0, mine)
    lax.fori_loop(1, n_slot, near_pairs, 0)
    lax.fori_loop(q_chunks, rs_chunks, upright_tables, 0)
    wait_bytes(rsb, rsem.at[3])
    part = sfb[p]
    for d in range(n_at - 1):
        part = part + rsb[d]
    agpart[...] = part * wtab[p // 2, 0:1, :]
    for d in range(1, n_at // 2 + 1):
        for dp in sorted({d, n_at - d}):
            send(agpart, agb.at[p], 4, dp, 0, group_r.at[own_group])
    keep = pltpu.make_async_copy(agpart, agb.at[p], group_r.at[own_group])
    keep.start()

    lax.fori_loop(rs_chunks, k_chunks, upright_tables, 0)

    total = jnp.zeros((8 * n_q, n_blk * bs), f32)
    for step in range(groups):
        this = lax.rem(own_group + step, groups)
        wait_bytes(agb.at[pl.ds(0, n_group)], group_r.at[this])
        for c in range(pair_k):
            at = pl.multiple_of(this * span_k + c * bs, bs)
            cos_part = agb[this * n_group + 2 * c]
            sin_part = agb[this * n_group + 2 * c + 1]
            ks = [nf[a : a + 1, pl.ds(at, bs)] * scales[a] for a in range(3)]
            rows = [cos_part] + [sin_part * k for k in ks]
            rows2 = [sin_part] + [cos_part * -k for k in ks]
            for kind, pieces in ((0, rows), (1, rows2)):
                place = slice(kind * span_k + c * bs, kind * span_k + (c + 1) * bs)
                high, low = split(jnp.concatenate(pieces, axis=0))
                rmat[step, 0 : 4 * n_q, place] = high
                rmat[step, 4 * n_q :, place] = low
        right = rmat[step]
        rows = pl.ds(pl.multiple_of(this * (4 * span_k), 4 * span_k), 4 * span_k)
        total = total + dot_nn(jnp.concatenate([right, right], axis=1), vmat[rows, :])
    total = total[0 : 4 * n_q] + total[4 * n_q :]
    folded = []
    for c in range(n_blk):
        folded.append(total[:, c * bs : (c + 1) * bs])
        cgs[c] = folded[c][0:n_q]
    for dq in range(1, n_k):
        send(cgs.at[lax.rem(q + dq, n_k)], cgr.at[dq - 1], 5, 0, dq)
    for c in range(n_blk):
        for a in range(3):
            product = qbuf[c] * folded[c][(1 + a) * n_q : (2 + a) * n_q]
            row = a * n_blk + c
            wf[row : row + 1, :] = jnp.sum(product, axis=0, keepdims=True)
    wait_bytes(cgr, rsem.at[5])
    charge_grad = cgs[q] + cgr[0]
    for dq in range(1, n_k - 1):
        charge_grad = charge_grad + cgr[dq]
    g_two = exact_tn(cw_ref[...], charge_grad) + short_grad

    for m in range(n_m):
        lanes = slice(m * bs, (m + 1) * bs)
        high, low = split(g_two * wcol2[0:n_f, m : m + 1])
        gwt[0:n_f, lanes] = high
        gwt[n_f:, lanes] = low
    twin = gwt[...]
    got = dot_nn(jnp.concatenate([twin, twin], axis=1), amat[...])
    got = got[0:n_f] + got[n_f:]
    for s in range(n_slot):
        tslot[s] = got[:, s * bs : (s + 1) * bs]
    tslot[n_slot] = jnp.zeros((n_f, bs), f32)
    for index, (dp, dq) in enumerate(near_peers):
        block = (1 + dp) * n_blk + lax.rem(q + dq, n_k)
        tsend[index] = tslot[inv[block]]
        send(tsend.at[index], trecv.at[index], 6, dp, dq)

    rows_c = 32
    rows_h = 16
    tile = 2 * bs
    tiles = wide_p // tile
    steps_p = bs // rows_c * tiles

    def pair_sums(grad, wd, values, last):
        twice = jnp.concatenate([grad, grad], axis=0).T
        for chunk in range(bs // rows_c):
            for m in range(n_m):
                start = (chunk * n_m + m) * rows_c
                rows = slice(start, start + rows_c)
                high, low = split(twice[chunk * rows_c : (chunk + 1) * rows_c] * wd[m : m + 1, :])
                gw[rows, 0 : 2 * n_f] = high
                gw[rows, 2 * n_f :] = low

        def product(step, buf):
            height = n_m * rows_c
            rows = pl.ds(pl.multiple_of(step // tiles * height, height), height)
            lanes = pl.ds(pl.multiple_of(lax.rem(step, tiles) * tile, tile), tile)
            buf[...] = dot_nn(gw[rows, :], values[:, lanes])

        def horner(step, buf):
            lanes = pl.ds(pl.multiple_of(lax.rem(step, tiles) * tile, tile), tile)
            for part in range(0, rows_c, rows_h):
                rows = pl.ds(pl.multiple_of(step // tiles * rows_c + part, rows_h), rows_h)

                def term(m):
                    return buf[m * rows_c + part : m * rows_c + part + rows_h, :]

                tau = geo[3, rows, lanes]
                tin = geo[4, rows, lanes]
                up = term(n_m - 1)
                up_d = up
                down = term(0)
                down_d = down
                for m in range(1, half_m):
                    down = down * tin + term(m)
                    down_d = down_d * tin + down
                    if m < half_m - 1:
                        up = up * tau + term(n_m - 1 - m)
                        up_d = up_d * tau + up
                up = up * tau + term(half_m)
                zero_sum = up + down * tin
                one_sum = up_d * tau - down_d * tin
                value = geo[5, rows, lanes] * zero_sum + geo[6, rows, lanes] * one_sum
                if last:
                    value = value + qsum[rows, lanes]
                qsum[rows, lanes] = value

        def both(turn, carry):
            step = 2 * turn
            product(step + 1, buf_b)
            horner(step, buf_a)
            product(step + 2, buf_a)
            horner(step + 1, buf_b)
            return carry

        product(0, buf_a)
        lax.fori_loop(0, steps_p // 2 - 1, both, 0)
        product(steps_p - 1, buf_b)
        horner(steps_p - 2, buf_a)
        horner(steps_p - 1, buf_b)

    pair_sums(g_two, wd2, zz, False)
    wait_bytes(trecv, rsem.at[6])
    g_one = g_two + tslot[0]
    for index in range(len(near_peers)):
        g_one = g_one + trecv[index]
    pair_sums(g_one, wd1, zf, True)

    own = [jnp.zeros((bs, bs), f32) for _ in range(3)]
    for s in range(n_slot):
        lanes = slice(s * bs, (s + 1) * bs)
        value = qsum[:, lanes]
        for a in range(3):
            product = value * geo[a, :, lanes]
            own[a] = own[a] + product
            pg[s, a : a + 1, :] = -jnp.sum(product, axis=0, keepdims=True)
    pg[n_slot, 0:3, :] = jnp.zeros((3, bs), f32)
    for a in range(3):
        pg[0, a : a + 1, :] = pg[0, a : a + 1, :] + jnp.sum(own[a].T, axis=0, keepdims=True)
    fsend[...] = jnp.zeros(fsend.shape, f32)
    for side in range(3):
        for c in range(n_blk):
            value = pg[inv[side * n_blk + c], 0:3, :]
            for a in range(3):
                row = a * n_blk + c
                piece = value[a : a + 1]
                if side == 1:
                    piece = piece + wf[row : row + 1, :]
                fsend[side, row : row + 1, :] = piece
    for index, (dp, dq) in enumerate(near_peers):
        send(fsend.at[1 + dp], frecv.at[index], 7, dp, dq)
    wait_bytes(frecv, rsem.at[7])
    force = fsend[1]
    for index in range(len(near_peers)):
        force = force + frecv[index]
    for a in range(3):
        for c in range(n_blk):
            row = a * n_blk + c
            out_ref[a : a + 1, c * bs : (c + 1) * bs] = -force[row : row + 1]

    wait_bytes(wide.at[pl.ds(0, 2 * n_blk)], ssem.at[0])
    wait_bytes(zwide.at[pl.ds(0, 3 * n_blk - 1)], ssem.at[1])
    wait_bytes(qbuf.at[pl.ds(0, n_k - 1)], ssem.at[2])
    wait_bytes(rsb, ssem.at[3])
    wait_bytes(agb.at[pl.ds(0, n_at - 1)], ssem.at[4])
    wait_bytes(cgr, ssem.at[5])
    wait_bytes(trecv, ssem.at[6])
    wait_bytes(frecv, ssem.at[7])


def body(
    n_at, n_k,
    positions, features, filter_one, filter_two, readout_in, readout_out, charge_weight,
    neighbour_blocks, live_slots, wave_ints,
):
    n_f = features.shape[0]
    n_m = filter_one.shape[0]
    n_q = charge_weight.shape[1]
    n_blk, n_slot = neighbour_blocks.shape
    bs = positions.shape[1] // n_blk
    n_wave = wave_ints.shape[1]
    local = n_blk * bs
    wide_n = n_slot * bs
    wide_p = (n_slot + n_slot % 2) * bs
    near_n = 3 * n_blk - 1
    k_chunks = n_wave // bs
    sizes = (n_at, n_k, n_blk, bs, n_slot, n_f, n_m, n_q, n_wave)
    v = pltpu.VMEM
    scratch = [
        v((3 * n_blk, n_f + 8, bs), f32),
        v((3 * n_blk, n_f, bs), f32),
        v((n_blk, bs, bs), f32),
        v((bs, bs), f32),
        v((bs, bs), f32),
        v((8, n_wave), f32),
        v((k_chunks, 8, bs), f32),
        v((2 * local, 2 * n_wave), bf16),
        v((4 * n_wave, local), bf16),
        v((2 * n_m * bs, wide_n), bf16),
        v((2 * wide_n, n_m * bs), bf16),
        v((4 * n_f, wide_p), bf16),
        v((4 * n_f, wide_p), bf16),
        v((7, bs, wide_p), f32),
        v((n_m, 2 * n_f), f32),
        v((n_m, 2 * n_f), f32),
        v((bs, bs), f32),
        v((bs, bs), f32),
        v((2 * n_f, n_m * bs), bf16),
        v((n_m * bs, 4 * n_f), bf16),
        v((n_m * 32, 2 * bs), f32),
        v((n_m * 32, 2 * bs), f32),
        v((bs, wide_p), f32),
        v((n_slot + 1, n_f, bs), f32),
        v((near_n, n_f, bs), f32),
        v((near_n, n_f, bs), f32),
        v((n_k, n_q, bs), f32),
        v((n_at, n_q, bs), f32),
        v((n_at - 1, n_q, bs), f32),
        v((n_at, n_q, bs), f32),
        v((n_q, bs), f32),
        v((n_at // n_group, 8 * n_q, n_group * bs), bf16),
        v((n_blk, n_q, bs), f32),
        v((n_k - 1, n_q, bs), f32),
        v((16, bs), f32),
        v((n_slot + 1, 8, bs), f32),
        v((3, 16, bs), f32),
        v((near_n, 16, bs), f32),
        pltpu.SMEM((3 * n_blk,), jnp.int32),
        pltpu.SemaphoreType.DMA((8,)),
        pltpu.SemaphoreType.DMA((8,)),
        pltpu.SemaphoreType.DMA((2,)),
        pltpu.SemaphoreType.DMA((n_at // n_group,)),
        pltpu.SemaphoreType.REGULAR((5,)),
    ]
    vmem = pl.BlockSpec(memory_space=pltpu.VMEM)
    smem = pl.BlockSpec(memory_space=pltpu.SMEM)
    return pl.pallas_call(
        functools.partial(kernel, sizes),
        out_shape=jax.ShapeDtypeStruct(positions.shape, f32),
        in_specs=[vmem] * 8 + [smem] * 2,
        out_specs=vmem,
        scratch_shapes=scratch,
        compiler_params=pltpu.CompilerParams(
            collective_id=0, has_side_effects=True, vmem_limit_bytes=56 * 2**20
        ),
    )(
        positions, features, filter_one, filter_two, readout_in,
        readout_out.reshape(1, n_f), charge_weight.T, wave_ints, neighbour_blocks, live_slots,
    )


def solution(mesh):
    in_specs = (
        P(None, "atoms"), P(None, "atoms"), P(), P(), P(), P(), P(),
        P("atoms", None), P("atoms"), P(None, "kvec"),
    )
    return jax.shard_map(
        functools.partial(body, mesh.shape["atoms"], mesh.shape["kvec"]),
        mesh=mesh, in_specs=in_specs, out_specs=P(None, "atoms"), check_vma=False,
    )
```

```python
import functools
import math

import jax
import jax.numpy as jnp
import numpy as np
from jax import lax
from jax.experimental import pallas as pl
from jax.experimental.pallas import tpu as pltpu
from jax.sharding import PartitionSpec as P

MESH = pl.DeviceIdType.MESH
highest = lax.Precision.HIGHEST
f32 = jnp.float32
bf16 = jnp.bfloat16
slab_width = 5.0
slab_height = 10.0
atom_density = 0.1
cutoff_radius = 5.0
self_offset = 0.0001
screen_square = 0.25
spread_square = 1.0
n_group = 8


def trig_coefficients():
    u = 0.5 * np.cos(np.pi * (np.arange(4000) + 0.5) / 8000)
    cheb = np.polynomial.chebyshev
    scaled = 8.0 * u * u - 1.0
    out = []
    for values, degree, weight in (
        (np.sin(2 * np.pi * u) / u, 6, u),
        (np.cos(2 * np.pi * u), 6, np.ones_like(u)),
    ):
        fitted = cheb.Chebyshev(cheb.chebfit(scaled, values, degree, w=weight))
        poly = fitted.convert(kind=np.polynomial.Polynomial)
        shifted = poly(np.polynomial.Polynomial([-1.0, 8.0]))
        out.append([float(c) for c in shifted.coef])
    return out


SIN_COEF, COS_COEF = trig_coefficients()


def sin_cos_turns(u):
    square = u * u
    sine = SIN_COEF[-1]
    for c in SIN_COEF[-2::-1]:
        sine = sine * square + c
    cosine = COS_COEF[-1]
    for c in COS_COEF[-2::-1]:
        cosine = cosine * square + c
    return sine * u, cosine


def split(x):
    high = x.astype(bf16)
    return high, (x - high.astype(f32)).astype(bf16)


def dot_nn(a, b):
    return lax.dot_general(a, b, (((1,), (0,)), ((), ())), preferred_element_type=f32)


def exact_nn(a, b):
    return lax.dot_general(
        a, b, (((1,), (0,)), ((), ())), precision=highest, preferred_element_type=f32
    )


def exact_tn(a, b):
    return lax.dot_general(
        a, b, (((0,), (0,)), ((), ())), precision=highest, preferred_element_type=f32
    )


def kernel(
    sizes,
    pos_ref, feat_ref, f1_ref, f2_ref, rin_ref, rout_ref, cw_ref, wave_ref, nb_ref, live_ref,
    out_ref,
    wide, zwide, post, xpad, own_t, nf, wtab, tab, vmat, amat, umat, zf, zz, geo,
    wd1, wd2, wcol1, wcol2, gwt, gw, buf_a, buf_b, qsum, tslot, tsend, trecv, qbuf, sfb, rsb, agb, agpart, rmat,
    cgs, cgr, wf, pg, fsend, frecv, inv,
    ssem, rsem, halo_r, group_r, greet_sem,
):
    n_at, n_k, n_blk, bs, n_slot, n_f, n_m, n_q, n_wave = sizes
    total_atoms = n_at * n_blk * bs
    p = lax.axis_index("atoms")
    q = lax.axis_index("kvec")
    half_m = n_m // 2
    wide_n = n_slot * bs
    k_chunks = n_wave // bs
    across = [(0, dq) for dq in range(1, n_k)]
    beside = [(1, 0), (-1, 0)]
    near_peers = [(dp, dq) for dq in range(1, n_k) for dp in (1, -1)] + across + beside

    def peer(dp, dq):
        return {"atoms": lax.rem(p + dp + n_at, n_at), "kvec": lax.rem(q + dq, n_k)}

    def send(src, dst, which, dp, dq, recv=None):
        copy = pltpu.make_async_remote_copy(
            src_ref=src, dst_ref=dst, send_sem=ssem.at[which],
            recv_sem=rsem.at[which] if recv is None else recv,
            device_id=peer(dp, dq), device_id_type=MESH,
        )
        copy.start()

    def wait_bytes(ref, sem):
        pltpu.make_async_copy(ref, ref, sem).wait()

    barrier = pltpu.get_barrier_semaphore()
    partners = across + beside
    for dp, dq in partners:
        pl.semaphore_signal(barrier, inc=1, device_id=peer(dp, dq), device_id_type=MESH)

    def greet(index, group):
        for dp, dq in group:
            pl.semaphore_signal(
                greet_sem.at[index], inc=1, device_id=peer(dp, dq), device_id_type=MESH
            )

    def met(index, group):
        pl.semaphore_wait(greet_sem.at[index], len(group))

    rounds = []
    reach = 1
    while reach < n_at // 2:
        rounds.append([(reach, 0), (-reach, 0)])
        reach *= 2

    for c in range(n_blk):
        lanes = slice(c * bs, (c + 1) * bs)
        wide[n_blk + c, 0:n_f, :] = feat_ref[:, lanes]
        wide[n_blk + c, n_f:, :] = jnp.zeros((8, bs), f32)
        wide[n_blk + c, n_f : n_f + 3, :] = pos_ref[:, lanes]
    pl.semaphore_wait(barrier, len(partners))
    own_rows = wide.at[pl.ds(n_blk, n_blk)]
    send(own_rows, wide.at[pl.ds(0, n_blk)], 0, 1, 0, halo_r.at[0])
    send(own_rows, wide.at[pl.ds(2 * n_blk, n_blk)], 0, -1, 0, halo_r.at[1])
    greet(0, across)
    greet(1, rounds[0])

    live = live_ref[q]
    mine = n_blk + q
    base = (p - 1) * n_blk
    total_blocks = n_at * n_blk

    def near_id(s):
        return jnp.minimum(lax.rem(nb_ref[q, s] - base + total_blocks, total_blocks), 3 * n_blk - 1)

    near = [near_id(s) for s in range(n_slot)]
    for c in range(3 * n_blk):
        found = jnp.int32(n_slot)
        for s in range(n_slot - 1, -1, -1):
            found = jnp.where((near[s] == c) & (s < live), s, found)
        inv[c] = found

    xpad[...] = jnp.zeros((bs, bs), f32)
    for c in range(n_blk):
        xpad[0:3, :] = pos_ref[:, c * bs : (c + 1) * bs]
        post[c] = xpad[...].T
    own_t[...] = post[q]

    steps = lax.broadcasted_iota(jnp.int32, (n_m, 2 * n_f), 0).astype(f32) - half_m
    gain = jnp.exp(-0.5 * steps * steps)
    for wd, src in ((wd1, f1_ref), (wd2, f2_ref)):
        wd[...] = jnp.concatenate([src[...], src[...]], axis=1) * gain
    for wcol, wd in ((wcol1, wd1), (wcol2, wd2)):
        xpad[0:n_m, :] = wd[...]
        wcol[...] = xpad[...].T

    nf[...] = jnp.zeros(nf.shape, f32)
    nf[0:3, :] = wave_ref[...].astype(f32)
    depth_side = n_blk * bs / (atom_density * slab_width * slab_height)
    sides = (slab_width * n_at, slab_height, depth_side)
    scales = [2.0 * math.pi / side for side in sides]
    kx, ky, kz = (nf[a : a + 1, :] * scales[a] for a in range(3))
    square = kx * kx + ky * ky + kz * kz
    weight = jnp.exp(-0.5 * spread_square * square) / (square + screen_square) * (2.0 / total_atoms)
    for c in range(k_chunks):
        wtab[c, 0:1, :] = weight[:, c * bs : (c + 1) * bs]

    rows_t = 16
    span = min(n_wave, 512)

    def tables(block):
        def one(step, carry):
            at = pl.multiple_of(step * rows_t, rows_t)
            cols = []
            for a in range(3):
                col = post[block, pl.ds(at, rows_t), a : a + 1] * (1.0 / sides[a])
                cols.append(col - jnp.round(col))
            row = pl.ds(pl.multiple_of(block * bs + at, rows_t), rows_t)
            low_row = pl.ds(pl.multiple_of((n_blk + block) * bs + at, rows_t), rows_t)
            for start in range(0, n_wave, span):
                lanes = slice(start, start + span)
                u = cols[0] * nf[0:1, lanes] + cols[1] * nf[1:2, lanes] + cols[2] * nf[2:3, lanes]
                sine, cosine = sin_cos_turns(u - jnp.round(u))
                tab[row, lanes], tab[low_row, lanes] = split(cosine)
                later = slice(n_wave + start, n_wave + start + span)
                tab[row, later], tab[low_row, later] = split(sine)
            return carry

        lax.fori_loop(0, bs // rows_t, one, 0)

    for block in range(n_blk // 2):
        tables(block)

    rows_g = 32
    centre = cutoff_radius * half_m / (n_m - 1)
    spacing = cutoff_radius / (n_m - 1)
    sharp = 0.5 / spacing ** 2

    def put_values(dest, value, lanes):
        high, low = split(value)
        dest[0:n_f, lanes] = high
        dest[n_f : 2 * n_f, lanes] = low
        dest[2 * n_f : 3 * n_f, lanes] = high
        dest[3 * n_f : 4 * n_f, lanes] = low

    def shape(dx, dy, dz, start, s, alive):
        squared = dx * dx + dy * dy + dz * dz + self_offset
        inverse = lax.rsqrt(squared)
        r = squared * inverse
        i = lax.broadcasted_iota(jnp.int32, (rows_g, bs), 0) + start
        j = lax.broadcasted_iota(jnp.int32, (rows_g, bs), 1)
        off = (i - j) * (i - j) + s
        active = jnp.where((r < cutoff_radius) & (off != 0), alive, 0.0)
        r = jnp.minimum(r, cutoff_radius)
        rho = r - centre
        bell = jnp.exp(-sharp * rho * rho)
        tau = jnp.exp((2.0 * sharp * spacing) * rho)
        tin = jnp.exp((-2.0 * sharp * spacing) * rho)
        sine, cosine = sin_cos_turns(r * (0.25 / cutoff_radius))
        cosine = cosine * active
        return active, inverse, rho, bell, tau, tin, sine, cosine, cosine * cosine

    def upright_pairs(s, block, high_at, low_at):
        lanes = pl.ds(pl.multiple_of(s * bs, bs), bs)
        alive = jnp.where(s < live, 1.0, 0.0).astype(f32)
        put_values(zf, wide[block, 0:n_f, :], lanes)
        left = wide[block, n_f : n_f + 8, :].T
        right = [wide[mine, n_f + a : n_f + a + 1, :] for a in range(3)]
        for start in range(0, bs, rows_g):
            rows = slice(start, start + rows_g)
            dx, dy, dz = (left[rows, a : a + 1] - right[a] for a in range(3))
            shaped = shape(dx, dy, dz, start, s, alive)
            bell, tau, tin, cut = shaped[3], shaped[4], shaped[5], shaped[8]
            first = cut * bell
            out = pl.ds(pl.multiple_of(high_at + start, rows_g), rows_g)
            low_out = pl.ds(pl.multiple_of(low_at + start, rows_g), rows_g)
            term = first
            for m in range(half_m, n_m):
                place = slice(m * bs, (m + 1) * bs)
                umat[out, place], umat[low_out, place] = split(term)
                term = term * tau
            term = first
            for m in range(half_m - 1, -1, -1):
                term = term * tin
                place = slice(m * bs, (m + 1) * bs)
                umat[out, place], umat[low_out, place] = split(term)

    def near_upright(s, carry):
        upright_pairs(s, near_id(s), (s + 1) * bs, (s + n_slot) * bs)
        return carry

    def pairs(s, block):
        lanes = pl.ds(pl.multiple_of(s * bs, bs), bs)
        alive = jnp.where(s < live, 1.0, 0.0).astype(f32)
        right = [wide[block, n_f + a : n_f + a + 1, :] for a in range(3)]
        for start in range(0, bs, rows_g):
            rows = slice(start, start + rows_g)
            dx, dy, dz = (own_t[rows, a : a + 1] - right[a] for a in range(3))
            active, inverse, rho, bell, tau, tin, sine, cosine, cut = shape(dx, dy, dz, start, s, alive)
            slope = (-math.pi / cutoff_radius) * sine * cosine
            first = cut * bell
            geo[0, rows, lanes] = dx
            geo[1, rows, lanes] = dy
            geo[2, rows, lanes] = dz
            geo[3, rows, lanes] = tau
            geo[4, rows, lanes] = tin
            geo[5, rows, lanes] = (slope - (2.0 * sharp) * rho * cut) * bell * inverse
            geo[6, rows, lanes] = (2.0 * sharp * spacing) * first * inverse
            term = first
            for m in range(half_m, n_m):
                out = slice(m * bs + start, m * bs + start + rows_g)
                low_out = slice(out.start + n_m * bs, out.stop + n_m * bs)
                amat[out, lanes], amat[low_out, lanes] = split(term)
                term = term * tau
            term = first
            for m in range(half_m - 1, -1, -1):
                term = term * tin
                out = slice(m * bs + start, m * bs + start + rows_g)
                low_out = slice(out.start + n_m * bs, out.stop + n_m * bs)
                amat[out, lanes], amat[low_out, lanes] = split(term)

    def near_pairs(s, carry):
        pairs(s, near_id(s))
        return carry

    group = 4

    def messages(values, wcol, lanes, total):
        stack = values[0 : 2 * n_f, lanes]
        stack = jnp.concatenate([stack, stack], axis=1)
        for g in range(0, n_m, group):
            place = slice(g * bs, (g + group) * bs)
            got = dot_nn(stack, umat[2 * lanes.start : 2 * lanes.stop, place])
            got = got[0:n_f] + got[n_f:]
            for m in range(group):
                weights = wcol[0:n_f, g + m : g + m + 1]
                total = total + got[:, m * bs : (m + 1) * bs] * weights
        return total

    first_lanes, later_lanes = slice(0, bs), slice(bs, wide_n)
    upright_pairs(0, mine, 0, bs)
    total = messages(zf, wcol1, first_lanes, wide[mine, 0:n_f, :])
    met(1, rounds[0])
    greet(2, rounds[1])
    wait_bytes(own_rows, halo_r.at[0])
    wait_bytes(own_rows, halo_r.at[1])
    lax.fori_loop(1, n_slot, near_upright, 0)
    met(2, rounds[1])
    greet(3, rounds[2])
    z_one = messages(zf, wcol1, later_lanes, total)
    zwide[mine] = z_one
    met(0, across)
    for dp, dq in near_peers:
        send(zwide.at[mine], zwide.at[(1 - dp) * n_blk + q], 1, dp, dq)
    for block in range(n_blk // 2, n_blk):
        tables(block)
    met(3, rounds[2])
    greet(4, rounds[3])
    put_values(zz, z_one, first_lanes)
    total = messages(zz, wcol2, first_lanes, z_one)
    wait_bytes(zwide.at[pl.ds(0, 3 * n_blk - 1)], rsem.at[1])
    for s in range(1, n_slot):
        put_values(zz, zwide[near[s]], slice(s * bs, (s + 1) * bs))
    z_two = messages(zz, wcol2, later_lanes, total)

    qbuf[q] = exact_nn(cw_ref[...], z_two)
    for dq in range(1, n_k):
        send(qbuf.at[q], qbuf.at[q], 2, 0, dq)
    hidden = exact_tn(rin_ref[...], z_two)
    gate = 1.0 / (1.0 + jnp.exp(-hidden))
    bent = gate * (1.0 + hidden * (1.0 - gate))
    short_grad = exact_nn(rin_ref[...] * rout_ref[...], bent)

    pair_k = n_group // 2
    span_k = pair_k * bs
    groups = n_at // n_group
    places = []
    for a in range(3):
        turns = pos_ref[a : a + 1, :] * (1.0 / sides[a])
        places.append(turns - jnp.round(turns))

    def upright_tables(chunk, carry):
        down = nf[:, pl.ds(pl.multiple_of(chunk * bs, bs), bs)].T
        at = (chunk // pair_k) * (4 * span_k) + lax.rem(chunk, pair_k) * bs
        for start in range(0, bs, rows_t):
            ks = [down[start : start + rows_t, a : a + 1] for a in range(3)]
            u = ks[0] * places[0] + ks[1] * places[1] + ks[2] * places[2]
            sine, cosine = sin_cos_turns(u - jnp.round(u))
            rows = [
                pl.ds(pl.multiple_of(at + part * span_k + start, rows_t), rows_t)
                for part in range(4)
            ]
            vmat[rows[0], :], vmat[rows[2], :] = split(cosine)
            vmat[rows[1], :], vmat[rows[3], :] = split(sine)
        return carry

    q_chunks, rs_chunks = k_chunks * 7 // 16, k_chunks * 10 // 16
    lax.fori_loop(0, q_chunks, upright_tables, 0)
    wait_bytes(qbuf.at[pl.ds(0, n_k - 1)], rsem.at[2])

    charges = jnp.concatenate([qbuf[c] for c in range(n_blk)], axis=1)
    stacked = jnp.concatenate(split(charges), axis=0)
    stacked = jnp.concatenate([stacked, stacked], axis=1)
    met(4, rounds[3])
    own_group, own_place = p // n_group, lax.rem(p, n_group)
    for step in range(groups):
        this = lax.rem(own_group + step, groups)
        for kind in range(2):
            lanes = pl.ds(pl.multiple_of(kind * n_wave + this * span_k, bs), span_k)
            got = dot_nn(stacked, tab[:, lanes])
            got = got[0:n_q] + got[n_q:]
            for c in range(pair_k):
                sfb[this * n_group + 2 * c + kind] = got[:, c * bs : (c + 1) * bs]
        for c in range(1 if step == 0 else 0, n_group):
            place = lax.rem(own_place + c, n_group)
            target = this * n_group + place
            ahead = lax.rem(target - p + n_at, n_at)
            send(sfb.at[target], rsb.at[ahead - 1], 3, ahead, 0)
    pairs(0, mine)
    lax.fori_loop(1, n_slot, near_pairs, 0)
    lax.fori_loop(q_chunks, rs_chunks, upright_tables, 0)
    wait_bytes(rsb, rsem.at[3])
    part = sfb[p]
    for d in range(n_at - 1):
        part = part + rsb[d]
    agpart[...] = part * wtab[p // 2, 0:1, :]
    for d in range(1, n_at // 2 + 1):
        for dp in sorted({d, n_at - d}):
            send(agpart, agb.at[p], 4, dp, 0, group_r.at[own_group])
    keep = pltpu.make_async_copy(agpart, agb.at[p], group_r.at[own_group])
    keep.start()

    lax.fori_loop(rs_chunks, k_chunks, upright_tables, 0)

    total = jnp.zeros((8 * n_q, n_blk * bs), f32)
    for step in range(groups):
        this = lax.rem(own_group + step, groups)
        wait_bytes(agb.at[pl.ds(0, n_group)], group_r.at[this])
        for c in range(pair_k):
            at = pl.multiple_of(this * span_k + c * bs, bs)
            cos_part = agb[this * n_group + 2 * c]
            sin_part = agb[this * n_group + 2 * c + 1]
            ks = [nf[a : a + 1, pl.ds(at, bs)] * scales[a] for a in range(3)]
            rows = [cos_part] + [sin_part * k for k in ks]
            rows2 = [sin_part] + [cos_part * -k for k in ks]
            for kind, pieces in ((0, rows), (1, rows2)):
                place = slice(kind * span_k + c * bs, kind * span_k + (c + 1) * bs)
                high, low = split(jnp.concatenate(pieces, axis=0))
                rmat[step, 0 : 4 * n_q, place] = high
                rmat[step, 4 * n_q :, place] = low
        right = rmat[step]
        rows = pl.ds(pl.multiple_of(this * (4 * span_k), 4 * span_k), 4 * span_k)
        total = total + dot_nn(jnp.concatenate([right, right], axis=1), vmat[rows, :])
    total = total[0 : 4 * n_q] + total[4 * n_q :]
    folded = []
    for c in range(n_blk):
        folded.append(total[:, c * bs : (c + 1) * bs])
        cgs[c] = folded[c][0:n_q]
    for dq in range(1, n_k):
        send(cgs.at[lax.rem(q + dq, n_k)], cgr.at[dq - 1], 5, 0, dq)
    for c in range(n_blk):
        for a in range(3):
            product = qbuf[c] * folded[c][(1 + a) * n_q : (2 + a) * n_q]
            row = a * n_blk + c
            wf[row : row + 1, :] = jnp.sum(product, axis=0, keepdims=True)
    wait_bytes(cgr, rsem.at[5])
    charge_grad = cgs[q] + cgr[0]
    for dq in range(1, n_k - 1):
        charge_grad = charge_grad + cgr[dq]
    g_two = exact_tn(cw_ref[...], charge_grad) + short_grad

    for m in range(n_m):
        lanes = slice(m * bs, (m + 1) * bs)
        high, low = split(g_two * wcol2[0:n_f, m : m + 1])
        gwt[0:n_f, lanes] = high
        gwt[n_f:, lanes] = low
    twin = gwt[...]
    got = dot_nn(jnp.concatenate([twin, twin], axis=1), amat[...])
    got = got[0:n_f] + got[n_f:]
    for s in range(n_slot):
        tslot[s] = got[:, s * bs : (s + 1) * bs]
    tslot[n_slot] = jnp.zeros((n_f, bs), f32)
    for index, (dp, dq) in enumerate(near_peers):
        block = (1 + dp) * n_blk + lax.rem(q + dq, n_k)
        tsend[index] = tslot[inv[block]]
        send(tsend.at[index], trecv.at[index], 6, dp, dq)

    rows_c = 16
    steps_p = bs // rows_c
    width = 3 * bs

    def pair_sums(grad, wd, values, last):
        twice = jnp.concatenate([grad, grad], axis=0).T
        for chunk in range(bs // rows_c):
            for m in range(n_m):
                start = (chunk * n_m + m) * rows_c
                rows = slice(start, start + rows_c)
                high, low = split(twice[chunk * rows_c : (chunk + 1) * rows_c] * wd[m : m + 1, :])
                gw[rows, 0 : 2 * n_f] = high
                gw[rows, 2 * n_f :] = low

        def product(step, buf):
            height = n_m * rows_c
            rows = pl.ds(pl.multiple_of(step * height, height), height)
            buf[...] = dot_nn(gw[rows, :], values[...])

        def horner(step, buf):
            rows = pl.ds(pl.multiple_of(step * rows_c, rows_c), rows_c)
            for start in range(0, wide_n, width):
                lanes = slice(start, min(start + width, wide_n))

                def term(m):
                    return buf[m * rows_c : (m + 1) * rows_c, lanes]

                tau = geo[3, rows, lanes]
                tin = geo[4, rows, lanes]
                up = term(n_m - 1)
                up_d = up
                down = term(0)
                down_d = down
                for m in range(1, half_m):
                    down = down * tin + term(m)
                    down_d = down_d * tin + down
                    if m < half_m - 1:
                        up = up * tau + term(n_m - 1 - m)
                        up_d = up_d * tau + up
                up = up * tau + term(half_m)
                zero_sum = up + down * tin
                one_sum = up_d * tau - down_d * tin
                value = geo[5, rows, lanes] * zero_sum + geo[6, rows, lanes] * one_sum
                if last:
                    value = value + qsum[rows, lanes]
                qsum[rows, lanes] = value

        def both(turn, carry):
            step = 2 * turn
            product(step + 1, buf_b)
            horner(step, buf_a)
            product(step + 2, buf_a)
            horner(step + 1, buf_b)
            return carry

        product(0, buf_a)
        lax.fori_loop(0, steps_p // 2 - 1, both, 0)
        product(steps_p - 1, buf_b)
        horner(steps_p - 2, buf_a)
        horner(steps_p - 1, buf_b)

    pair_sums(g_two, wd2, zz, False)
    wait_bytes(trecv, rsem.at[6])
    g_one = g_two + tslot[0]
    for index in range(len(near_peers)):
        g_one = g_one + trecv[index]
    pair_sums(g_one, wd1, zf, True)

    own = [jnp.zeros((bs, bs), f32) for _ in range(3)]
    for s in range(n_slot):
        lanes = slice(s * bs, (s + 1) * bs)
        value = qsum[:, lanes]
        for a in range(3):
            product = value * geo[a, :, lanes]
            own[a] = own[a] + product
            pg[s, a : a + 1, :] = -jnp.sum(product, axis=0, keepdims=True)
    pg[n_slot, 0:3, :] = jnp.zeros((3, bs), f32)
    for a in range(3):
        pg[0, a : a + 1, :] = pg[0, a : a + 1, :] + jnp.sum(own[a].T, axis=0, keepdims=True)
    fsend[...] = jnp.zeros(fsend.shape, f32)
    for side in range(3):
        for c in range(n_blk):
            value = pg[inv[side * n_blk + c], 0:3, :]
            for a in range(3):
                row = a * n_blk + c
                piece = value[a : a + 1]
                if side == 1:
                    piece = piece + wf[row : row + 1, :]
                fsend[side, row : row + 1, :] = piece
    for index, (dp, dq) in enumerate(near_peers):
        send(fsend.at[1 + dp], frecv.at[index], 7, dp, dq)
    wait_bytes(frecv, rsem.at[7])
    force = fsend[1]
    for index in range(len(near_peers)):
        force = force + frecv[index]
    for a in range(3):
        for c in range(n_blk):
            row = a * n_blk + c
            out_ref[a : a + 1, c * bs : (c + 1) * bs] = -force[row : row + 1]

    wait_bytes(wide.at[pl.ds(0, 2 * n_blk)], ssem.at[0])
    wait_bytes(zwide.at[pl.ds(0, 3 * n_blk - 1)], ssem.at[1])
    wait_bytes(qbuf.at[pl.ds(0, n_k - 1)], ssem.at[2])
    wait_bytes(rsb, ssem.at[3])
    wait_bytes(agb.at[pl.ds(0, n_at - 1)], ssem.at[4])
    wait_bytes(cgr, ssem.at[5])
    wait_bytes(trecv, ssem.at[6])
    wait_bytes(frecv, ssem.at[7])


def body(
    n_at, n_k,
    positions, features, filter_one, filter_two, readout_in, readout_out, charge_weight,
    neighbour_blocks, live_slots, wave_ints,
):
    n_f = features.shape[0]
    n_m = filter_one.shape[0]
    n_q = charge_weight.shape[1]
    n_blk, n_slot = neighbour_blocks.shape
    bs = positions.shape[1] // n_blk
    n_wave = wave_ints.shape[1]
    local = n_blk * bs
    wide_n = n_slot * bs
    near_n = 3 * n_blk - 1
    k_chunks = n_wave // bs
    sizes = (n_at, n_k, n_blk, bs, n_slot, n_f, n_m, n_q, n_wave)
    v = pltpu.VMEM
    scratch = [
        v((3 * n_blk, n_f + 8, bs), f32),
        v((3 * n_blk, n_f, bs), f32),
        v((n_blk, bs, bs), f32),
        v((bs, bs), f32),
        v((bs, bs), f32),
        v((8, n_wave), f32),
        v((k_chunks, 8, bs), f32),
        v((2 * local, 2 * n_wave), bf16),
        v((4 * n_wave, local), bf16),
        v((2 * n_m * bs, wide_n), bf16),
        v((2 * wide_n, n_m * bs), bf16),
        v((4 * n_f, wide_n), bf16),
        v((4 * n_f, wide_n), bf16),
        v((7, bs, wide_n), f32),
        v((n_m, 2 * n_f), f32),
        v((n_m, 2 * n_f), f32),
        v((bs, bs), f32),
        v((bs, bs), f32),
        v((2 * n_f, n_m * bs), bf16),
        v((n_m * bs, 4 * n_f), bf16),
        v((n_m * 16, wide_n), f32),
        v((n_m * 16, wide_n), f32),
        v((bs, wide_n), f32),
        v((n_slot + 1, n_f, bs), f32),
        v((near_n, n_f, bs), f32),
        v((near_n, n_f, bs), f32),
        v((n_k, n_q, bs), f32),
        v((n_at, n_q, bs), f32),
        v((n_at - 1, n_q, bs), f32),
        v((n_at, n_q, bs), f32),
        v((n_q, bs), f32),
        v((n_at // n_group, 8 * n_q, n_group * bs), bf16),
        v((n_blk, n_q, bs), f32),
        v((n_k - 1, n_q, bs), f32),
        v((16, bs), f32),
        v((n_slot + 1, 8, bs), f32),
        v((3, 16, bs), f32),
        v((near_n, 16, bs), f32),
        pltpu.SMEM((3 * n_blk,), jnp.int32),
        pltpu.SemaphoreType.DMA((8,)),
        pltpu.SemaphoreType.DMA((8,)),
        pltpu.SemaphoreType.DMA((2,)),
        pltpu.SemaphoreType.DMA((n_at // n_group,)),
        pltpu.SemaphoreType.REGULAR((5,)),
    ]
    vmem = pl.BlockSpec(memory_space=pltpu.VMEM)
    smem = pl.BlockSpec(memory_space=pltpu.SMEM)
    return pl.pallas_call(
        functools.partial(kernel, sizes),
        out_shape=jax.ShapeDtypeStruct(positions.shape, f32),
        in_specs=[vmem] * 8 + [smem] * 2,
        out_specs=vmem,
        scratch_shapes=scratch,
        compiler_params=pltpu.CompilerParams(
            collective_id=0, has_side_effects=True, vmem_limit_bytes=56 * 2**20
        ),
    )(
        positions, features, filter_one, filter_two, readout_in,
        readout_out.reshape(1, n_f), charge_weight.T, wave_ints, neighbour_blocks, live_slots,
    )


def solution(mesh):
    in_specs = (
        P(None, "atoms"), P(None, "atoms"), P(), P(), P(), P(), P(),
        P("atoms", None), P("atoms"), P(None, "kvec"),
    )
    return jax.shard_map(
        functools.partial(body, mesh.shape["atoms"], mesh.shape["kvec"]),
        mesh=mesh, in_specs=in_specs, out_specs=P(None, "atoms"), check_vma=False,
    )
```

```python
import functools
import math

import jax
import jax.numpy as jnp
import numpy as np
from jax import lax
from jax.experimental import pallas as pl
from jax.experimental.pallas import tpu as pltpu
from jax.sharding import PartitionSpec as P

MESH = pl.DeviceIdType.MESH
highest = lax.Precision.HIGHEST
f32 = jnp.float32
bf16 = jnp.bfloat16
slab_width = 5.0
slab_height = 10.0
atom_density = 0.1
cutoff_radius = 5.0
self_offset = 0.0001
screen_square = 0.25
spread_square = 1.0
n_group = 8


def trig_coefficients():
    u = 0.5 * np.cos(np.pi * (np.arange(4000) + 0.5) / 8000)
    cheb = np.polynomial.chebyshev
    scaled = 8.0 * u * u - 1.0
    out = []
    for values, degree, weight in (
        (np.sin(2 * np.pi * u) / u, 6, u),
        (np.cos(2 * np.pi * u), 6, np.ones_like(u)),
    ):
        fitted = cheb.Chebyshev(cheb.chebfit(scaled, values, degree, w=weight))
        poly = fitted.convert(kind=np.polynomial.Polynomial)
        shifted = poly(np.polynomial.Polynomial([-1.0, 8.0]))
        out.append([float(c) for c in shifted.coef])
    return out


SIN_COEF, COS_COEF = trig_coefficients()


def sin_cos_turns(u):
    square = u * u
    sine = SIN_COEF[-1]
    for c in SIN_COEF[-2::-1]:
        sine = sine * square + c
    cosine = COS_COEF[-1]
    for c in COS_COEF[-2::-1]:
        cosine = cosine * square + c
    return sine * u, cosine


def split(x):
    high = x.astype(bf16)
    return high, (x - high.astype(f32)).astype(bf16)


def dot_nn(a, b):
    return lax.dot_general(a, b, (((1,), (0,)), ((), ())), preferred_element_type=f32)


def exact_nn(a, b):
    return lax.dot_general(
        a, b, (((1,), (0,)), ((), ())), precision=highest, preferred_element_type=f32
    )


def exact_tn(a, b):
    return lax.dot_general(
        a, b, (((0,), (0,)), ((), ())), precision=highest, preferred_element_type=f32
    )


def kernel(
    sizes,
    pos_ref, feat_ref, f1_ref, f2_ref, rin_ref, rout_ref, cw_ref, wave_ref, nb_ref, live_ref,
    out_ref,
    wide, zwide, post, xpad, own_t, nf, wtab, tab, vmat, amat, umat, zf, zz, geo,
    wd1, wd2, wcol1, wcol2, gwt, gw, buf_a, buf_b, qsum, tslot, tsend, trecv, qbuf, sfb, rsb, agb, agpart, rmat,
    cgs, cgr, wf, pg, fsend, frecv, inv,
    ssem, rsem, halo_r, group_r, greet_sem,
):
    n_at, n_k, n_blk, bs, n_slot, n_f, n_m, n_q, n_wave = sizes
    total_atoms = n_at * n_blk * bs
    p = lax.axis_index("atoms")
    q = lax.axis_index("kvec")
    half_m = n_m // 2
    wide_n = n_slot * bs
    k_chunks = n_wave // bs
    across = [(0, dq) for dq in range(1, n_k)]
    beside = [(1, 0), (-1, 0)]
    near_peers = [(dp, dq) for dq in range(1, n_k) for dp in (1, -1)] + across + beside

    def peer(dp, dq):
        return {"atoms": lax.rem(p + dp + n_at, n_at), "kvec": lax.rem(q + dq, n_k)}

    def send(src, dst, which, dp, dq, recv=None):
        copy = pltpu.make_async_remote_copy(
            src_ref=src, dst_ref=dst, send_sem=ssem.at[which],
            recv_sem=rsem.at[which] if recv is None else recv,
            device_id=peer(dp, dq), device_id_type=MESH,
        )
        copy.start()

    def wait_bytes(ref, sem):
        pltpu.make_async_copy(ref, ref, sem).wait()

    barrier = pltpu.get_barrier_semaphore()
    partners = across + beside
    for dp, dq in partners:
        pl.semaphore_signal(barrier, inc=1, device_id=peer(dp, dq), device_id_type=MESH)

    def greet(index, group):
        for dp, dq in group:
            pl.semaphore_signal(
                greet_sem.at[index], inc=1, device_id=peer(dp, dq), device_id_type=MESH
            )

    def met(index, group):
        pl.semaphore_wait(greet_sem.at[index], len(group))

    rounds = []
    reach = 1
    while reach < n_at // 2:
        rounds.append([(reach, 0), (-reach, 0)])
        reach *= 2

    for c in range(n_blk):
        lanes = slice(c * bs, (c + 1) * bs)
        wide[n_blk + c, 0:n_f, :] = feat_ref[:, lanes]
        wide[n_blk + c, n_f:, :] = jnp.zeros((8, bs), f32)
        wide[n_blk + c, n_f : n_f + 3, :] = pos_ref[:, lanes]
    pl.semaphore_wait(barrier, len(partners))
    own_rows = wide.at[pl.ds(n_blk, n_blk)]
    send(own_rows, wide.at[pl.ds(0, n_blk)], 0, 1, 0, halo_r.at[0])
    send(own_rows, wide.at[pl.ds(2 * n_blk, n_blk)], 0, -1, 0, halo_r.at[1])
    greet(0, across)
    greet(1, rounds[0])

    live = live_ref[q]
    mine = n_blk + q
    base = (p - 1) * n_blk
    total_blocks = n_at * n_blk

    def near_id(s):
        return jnp.minimum(lax.rem(nb_ref[q, s] - base + total_blocks, total_blocks), 3 * n_blk - 1)

    near = [near_id(s) for s in range(n_slot)]
    for c in range(3 * n_blk):
        found = jnp.int32(n_slot)
        for s in range(n_slot - 1, -1, -1):
            found = jnp.where((near[s] == c) & (s < live), s, found)
        inv[c] = found

    xpad[...] = jnp.zeros((bs, bs), f32)
    for c in range(n_blk):
        xpad[0:3, :] = pos_ref[:, c * bs : (c + 1) * bs]
        post[c] = xpad[...].T
    own_t[...] = post[q]

    steps = lax.broadcasted_iota(jnp.int32, (n_m, 2 * n_f), 0).astype(f32) - half_m
    gain = jnp.exp(-0.5 * steps * steps)
    for wd, src in ((wd1, f1_ref), (wd2, f2_ref)):
        wd[...] = jnp.concatenate([src[...], src[...]], axis=1) * gain
    for wcol, wd in ((wcol1, wd1), (wcol2, wd2)):
        xpad[0:n_m, :] = wd[...]
        wcol[...] = xpad[...].T

    nf[...] = jnp.zeros(nf.shape, f32)
    nf[0:3, :] = wave_ref[...].astype(f32)
    depth_side = n_blk * bs / (atom_density * slab_width * slab_height)
    sides = (slab_width * n_at, slab_height, depth_side)
    scales = [2.0 * math.pi / side for side in sides]
    kx, ky, kz = (nf[a : a + 1, :] * scales[a] for a in range(3))
    square = kx * kx + ky * ky + kz * kz
    weight = jnp.exp(-0.5 * spread_square * square) / (square + screen_square) * (2.0 / total_atoms)
    for c in range(k_chunks):
        wtab[c, 0:1, :] = weight[:, c * bs : (c + 1) * bs]

    rows_t = 16
    span = min(n_wave, 512)

    def tables(block):
        def one(step, carry):
            at = pl.multiple_of(step * rows_t, rows_t)
            cols = []
            for a in range(3):
                col = post[block, pl.ds(at, rows_t), a : a + 1] * (1.0 / sides[a])
                cols.append(col - jnp.round(col))
            row = pl.ds(pl.multiple_of(block * bs + at, rows_t), rows_t)
            low_row = pl.ds(pl.multiple_of((n_blk + block) * bs + at, rows_t), rows_t)
            for start in range(0, n_wave, span):
                lanes = slice(start, start + span)
                u = cols[0] * nf[0:1, lanes] + cols[1] * nf[1:2, lanes] + cols[2] * nf[2:3, lanes]
                sine, cosine = sin_cos_turns(u - jnp.round(u))
                tab[row, lanes], tab[low_row, lanes] = split(cosine)
                later = slice(n_wave + start, n_wave + start + span)
                tab[row, later], tab[low_row, later] = split(sine)
            return carry

        lax.fori_loop(0, bs // rows_t, one, 0)

    for block in range(n_blk // 2):
        tables(block)

    rows_g = 32
    centre = cutoff_radius * half_m / (n_m - 1)
    spacing = cutoff_radius / (n_m - 1)
    sharp = 0.5 / spacing ** 2

    def put_values(dest, value, lanes):
        high, low = split(value)
        dest[0:n_f, lanes] = high
        dest[n_f : 2 * n_f, lanes] = low
        dest[2 * n_f : 3 * n_f, lanes] = high
        dest[3 * n_f : 4 * n_f, lanes] = low

    def shape(dx, dy, dz, start, s, alive):
        squared = dx * dx + dy * dy + dz * dz + self_offset
        inverse = lax.rsqrt(squared)
        r = squared * inverse
        i = lax.broadcasted_iota(jnp.int32, (rows_g, bs), 0) + start
        j = lax.broadcasted_iota(jnp.int32, (rows_g, bs), 1)
        off = (i - j) * (i - j) + s
        active = jnp.where((r < cutoff_radius) & (off != 0), alive, 0.0)
        r = jnp.minimum(r, cutoff_radius)
        rho = r - centre
        bell = jnp.exp(-sharp * rho * rho)
        tau = jnp.exp((2.0 * sharp * spacing) * rho)
        tin = jnp.exp((-2.0 * sharp * spacing) * rho)
        sine, cosine = sin_cos_turns(r * (0.25 / cutoff_radius))
        cosine = cosine * active
        return active, inverse, rho, bell, tau, tin, sine, cosine, cosine * cosine

    def upright_pairs(s, block, high_at, low_at):
        lanes = pl.ds(pl.multiple_of(s * bs, bs), bs)
        alive = jnp.where(s < live, 1.0, 0.0).astype(f32)
        put_values(zf, wide[block, 0:n_f, :], lanes)
        left = wide[block, n_f : n_f + 8, :].T
        right = [wide[mine, n_f + a : n_f + a + 1, :] for a in range(3)]
        for start in range(0, bs, rows_g):
            rows = slice(start, start + rows_g)
            dx, dy, dz = (left[rows, a : a + 1] - right[a] for a in range(3))
            shaped = shape(dx, dy, dz, start, s, alive)
            bell, tau, tin, cut = shaped[3], shaped[4], shaped[5], shaped[8]
            first = cut * bell
            out = pl.ds(pl.multiple_of(high_at + start, rows_g), rows_g)
            low_out = pl.ds(pl.multiple_of(low_at + start, rows_g), rows_g)
            term = first
            for m in range(half_m, n_m):
                place = slice(m * bs, (m + 1) * bs)
                umat[out, place], umat[low_out, place] = split(term)
                term = term * tau
            term = first
            for m in range(half_m - 1, -1, -1):
                term = term * tin
                place = slice(m * bs, (m + 1) * bs)
                umat[out, place], umat[low_out, place] = split(term)

    def near_upright(s, carry):
        upright_pairs(s, near_id(s), (s + 1) * bs, (s + n_slot) * bs)
        return carry

    def pairs(s, block):
        lanes = pl.ds(pl.multiple_of(s * bs, bs), bs)
        alive = jnp.where(s < live, 1.0, 0.0).astype(f32)
        right = [wide[block, n_f + a : n_f + a + 1, :] for a in range(3)]
        for start in range(0, bs, rows_g):
            rows = slice(start, start + rows_g)
            dx, dy, dz = (own_t[rows, a : a + 1] - right[a] for a in range(3))
            active, inverse, rho, bell, tau, tin, sine, cosine, cut = shape(dx, dy, dz, start, s, alive)
            slope = (-math.pi / cutoff_radius) * sine * cosine
            first = cut * bell
            geo[0, rows, lanes] = dx
            geo[1, rows, lanes] = dy
            geo[2, rows, lanes] = dz
            geo[3, rows, lanes] = tau
            geo[4, rows, lanes] = tin
            geo[5, rows, lanes] = (slope - (2.0 * sharp) * rho * cut) * bell * inverse
            geo[6, rows, lanes] = (2.0 * sharp * spacing) * first * inverse
            term = first
            for m in range(half_m, n_m):
                out = slice(m * bs + start, m * bs + start + rows_g)
                low_out = slice(out.start + n_m * bs, out.stop + n_m * bs)
                amat[out, lanes], amat[low_out, lanes] = split(term)
                term = term * tau
            term = first
            for m in range(half_m - 1, -1, -1):
                term = term * tin
                out = slice(m * bs + start, m * bs + start + rows_g)
                low_out = slice(out.start + n_m * bs, out.stop + n_m * bs)
                amat[out, lanes], amat[low_out, lanes] = split(term)

    def near_pairs(s, carry):
        pairs(s, near_id(s))
        return carry

    group = 4

    def messages(values, wcol, lanes, total):
        stack = values[0 : 2 * n_f, lanes]
        stack = jnp.concatenate([stack, stack], axis=1)
        for g in range(0, n_m, group):
            place = slice(g * bs, (g + group) * bs)
            got = dot_nn(stack, umat[2 * lanes.start : 2 * lanes.stop, place])
            got = got[0:n_f] + got[n_f:]
            for m in range(group):
                weights = wcol[0:n_f, g + m : g + m + 1]
                total = total + got[:, m * bs : (m + 1) * bs] * weights
        return total

    first_lanes, later_lanes = slice(0, bs), slice(bs, wide_n)
    upright_pairs(0, mine, 0, bs)
    total = messages(zf, wcol1, first_lanes, wide[mine, 0:n_f, :])
    met(1, rounds[0])
    greet(2, rounds[1])
    wait_bytes(own_rows, halo_r.at[0])
    wait_bytes(own_rows, halo_r.at[1])
    lax.fori_loop(1, n_slot, near_upright, 0)
    met(2, rounds[1])
    greet(3, rounds[2])
    z_one = messages(zf, wcol1, later_lanes, total)
    zwide[mine] = z_one
    met(0, across)
    for dp, dq in near_peers:
        send(zwide.at[mine], zwide.at[(1 - dp) * n_blk + q], 1, dp, dq)
    for block in range(n_blk // 2, n_blk):
        tables(block)
    met(3, rounds[2])
    greet(4, rounds[3])
    put_values(zz, z_one, first_lanes)
    total = messages(zz, wcol2, first_lanes, z_one)
    wait_bytes(zwide.at[pl.ds(0, 3 * n_blk - 1)], rsem.at[1])
    for s in range(1, n_slot):
        put_values(zz, zwide[near[s]], slice(s * bs, (s + 1) * bs))
    z_two = messages(zz, wcol2, later_lanes, total)

    qbuf[q] = exact_nn(cw_ref[...], z_two)
    for dq in range(1, n_k):
        send(qbuf.at[q], qbuf.at[q], 2, 0, dq)
    hidden = exact_tn(rin_ref[...], z_two)
    gate = 1.0 / (1.0 + jnp.exp(-hidden))
    bent = gate * (1.0 + hidden * (1.0 - gate))
    short_grad = exact_nn(rin_ref[...] * rout_ref[...], bent)

    pair_k = n_group // 2
    span_k = pair_k * bs
    groups = n_at // n_group
    places = []
    for a in range(3):
        turns = pos_ref[a : a + 1, :] * (1.0 / sides[a])
        places.append(turns - jnp.round(turns))

    def upright_tables(chunk, carry):
        down = nf[:, pl.ds(pl.multiple_of(chunk * bs, bs), bs)].T
        at = (chunk // pair_k) * (4 * span_k) + lax.rem(chunk, pair_k) * bs
        for start in range(0, bs, rows_t):
            ks = [down[start : start + rows_t, a : a + 1] for a in range(3)]
            u = ks[0] * places[0] + ks[1] * places[1] + ks[2] * places[2]
            sine, cosine = sin_cos_turns(u - jnp.round(u))
            rows = [
                pl.ds(pl.multiple_of(at + part * span_k + start, rows_t), rows_t)
                for part in range(4)
            ]
            vmat[rows[0], :], vmat[rows[2], :] = split(cosine)
            vmat[rows[1], :], vmat[rows[3], :] = split(sine)
        return carry

    q_chunks, rs_chunks = k_chunks * 7 // 16, k_chunks * 10 // 16
    lax.fori_loop(0, q_chunks, upright_tables, 0)
    wait_bytes(qbuf.at[pl.ds(0, n_k - 1)], rsem.at[2])

    charges = jnp.concatenate([qbuf[c] for c in range(n_blk)], axis=1)
    stacked = jnp.concatenate(split(charges), axis=0)
    stacked = jnp.concatenate([stacked, stacked], axis=1)
    met(4, rounds[3])
    own_group, own_place = p // n_group, lax.rem(p, n_group)
    for step in range(groups):
        this = lax.rem(own_group + step, groups)
        for kind in range(2):
            lanes = pl.ds(pl.multiple_of(kind * n_wave + this * span_k, bs), span_k)
            got = dot_nn(stacked, tab[:, lanes])
            got = got[0:n_q] + got[n_q:]
            for c in range(pair_k):
                sfb[this * n_group + 2 * c + kind] = got[:, c * bs : (c + 1) * bs]
        for c in range(1 if step == 0 else 0, n_group):
            place = lax.rem(own_place + c, n_group)
            target = this * n_group + place
            ahead = lax.rem(target - p + n_at, n_at)
            send(sfb.at[target], rsb.at[ahead - 1], 3, ahead, 0)
    pairs(0, mine)
    lax.fori_loop(1, n_slot, near_pairs, 0)
    lax.fori_loop(q_chunks, rs_chunks, upright_tables, 0)
    wait_bytes(rsb, rsem.at[3])
    part = sfb[p]
    for d in range(n_at - 1):
        part = part + rsb[d]
    agpart[...] = part * wtab[p // 2, 0:1, :]
    for d in range(1, n_at // 2 + 1):
        for dp in sorted({d, n_at - d}):
            send(agpart, agb.at[p], 4, dp, 0, group_r.at[own_group])
    keep = pltpu.make_async_copy(agpart, agb.at[p], group_r.at[own_group])
    keep.start()

    lax.fori_loop(rs_chunks, k_chunks, upright_tables, 0)

    total = jnp.zeros((8 * n_q, n_blk * bs), f32)
    for step in range(groups):
        this = lax.rem(own_group + step, groups)
        wait_bytes(agb.at[pl.ds(0, n_group)], group_r.at[this])
        for c in range(pair_k):
            at = pl.multiple_of(this * span_k + c * bs, bs)
            cos_part = agb[this * n_group + 2 * c]
            sin_part = agb[this * n_group + 2 * c + 1]
            ks = [nf[a : a + 1, pl.ds(at, bs)] * scales[a] for a in range(3)]
            rows = [cos_part] + [sin_part * k for k in ks]
            rows2 = [sin_part] + [cos_part * -k for k in ks]
            for kind, pieces in ((0, rows), (1, rows2)):
                place = slice(kind * span_k + c * bs, kind * span_k + (c + 1) * bs)
                high, low = split(jnp.concatenate(pieces, axis=0))
                rmat[step, 0 : 4 * n_q, place] = high
                rmat[step, 4 * n_q :, place] = low
        right = rmat[step]
        rows = pl.ds(pl.multiple_of(this * (4 * span_k), 4 * span_k), 4 * span_k)
        total = total + dot_nn(jnp.concatenate([right, right], axis=1), vmat[rows, :])
    total = total[0 : 4 * n_q] + total[4 * n_q :]
    folded = []
    for c in range(n_blk):
        folded.append(total[:, c * bs : (c + 1) * bs])
        cgs[c] = folded[c][0:n_q]
    for dq in range(1, n_k):
        send(cgs.at[lax.rem(q + dq, n_k)], cgr.at[dq - 1], 5, 0, dq)
    for c in range(n_blk):
        for a in range(3):
            product = qbuf[c] * folded[c][(1 + a) * n_q : (2 + a) * n_q]
            row = a * n_blk + c
            wf[row : row + 1, :] = jnp.sum(product, axis=0, keepdims=True)
    wait_bytes(cgr, rsem.at[5])
    charge_grad = cgs[q] + cgr[0]
    for dq in range(1, n_k - 1):
        charge_grad = charge_grad + cgr[dq]
    g_two = exact_tn(cw_ref[...], charge_grad) + short_grad

    for m in range(n_m):
        lanes = slice(m * bs, (m + 1) * bs)
        high, low = split(g_two * wcol2[0:n_f, m : m + 1])
        gwt[0:n_f, lanes] = high
        gwt[n_f:, lanes] = low
    twin = gwt[...]
    got = dot_nn(jnp.concatenate([twin, twin], axis=1), amat[...])
    got = got[0:n_f] + got[n_f:]
    for s in range(n_slot):
        tslot[s] = got[:, s * bs : (s + 1) * bs]
    tslot[n_slot] = jnp.zeros((n_f, bs), f32)
    for index, (dp, dq) in enumerate(near_peers):
        block = (1 + dp) * n_blk + lax.rem(q + dq, n_k)
        tsend[index] = tslot[inv[block]]
        send(tsend.at[index], trecv.at[index], 6, dp, dq)

    rows_c = 32
    steps_p = bs // rows_c
    width = bs

    def pair_sums(grad, wd, values, last):
        twice = jnp.concatenate([grad, grad], axis=0).T
        for chunk in range(bs // rows_c):
            for m in range(n_m):
                start = (chunk * n_m + m) * rows_c
                rows = slice(start, start + rows_c)
                high, low = split(twice[chunk * rows_c : (chunk + 1) * rows_c] * wd[m : m + 1, :])
                gw[rows, 0 : 2 * n_f] = high
                gw[rows, 2 * n_f :] = low

        def product(step, buf):
            height = n_m * rows_c
            rows = pl.ds(pl.multiple_of(step * height, height), height)
            buf[...] = dot_nn(gw[rows, :], values[...])

        def horner(step, buf):
            rows = pl.ds(pl.multiple_of(step * rows_c, rows_c), rows_c)
            for start in range(0, wide_n, width):
                lanes = slice(start, min(start + width, wide_n))

                def term(m):
                    return buf[m * rows_c : (m + 1) * rows_c, lanes]

                tau = geo[3, rows, lanes]
                tin = geo[4, rows, lanes]
                up = term(n_m - 1)
                up_d = up
                down = term(0)
                down_d = down
                for m in range(1, half_m):
                    down = down * tin + term(m)
                    down_d = down_d * tin + down
                    if m < half_m - 1:
                        up = up * tau + term(n_m - 1 - m)
                        up_d = up_d * tau + up
                up = up * tau + term(half_m)
                zero_sum = up + down * tin
                one_sum = up_d * tau - down_d * tin
                value = geo[5, rows, lanes] * zero_sum + geo[6, rows, lanes] * one_sum
                if last:
                    value = value + qsum[rows, lanes]
                qsum[rows, lanes] = value

        def both(turn, carry):
            step = 2 * turn
            product(step + 1, buf_b)
            horner(step, buf_a)
            product(step + 2, buf_a)
            horner(step + 1, buf_b)
            return carry

        product(0, buf_a)
        lax.fori_loop(0, steps_p // 2 - 1, both, 0)
        product(steps_p - 1, buf_b)
        horner(steps_p - 2, buf_a)
        horner(steps_p - 1, buf_b)

    pair_sums(g_two, wd2, zz, False)
    wait_bytes(trecv, rsem.at[6])
    g_one = g_two + tslot[0]
    for index in range(len(near_peers)):
        g_one = g_one + trecv[index]
    pair_sums(g_one, wd1, zf, True)

    own = [jnp.zeros((bs, bs), f32) for _ in range(3)]
    for s in range(n_slot):
        lanes = slice(s * bs, (s + 1) * bs)
        value = qsum[:, lanes]
        for a in range(3):
            product = value * geo[a, :, lanes]
            own[a] = own[a] + product
            pg[s, a : a + 1, :] = -jnp.sum(product, axis=0, keepdims=True)
    pg[n_slot, 0:3, :] = jnp.zeros((3, bs), f32)
    for a in range(3):
        pg[0, a : a + 1, :] = pg[0, a : a + 1, :] + jnp.sum(own[a].T, axis=0, keepdims=True)
    fsend[...] = jnp.zeros(fsend.shape, f32)
    for side in range(3):
        for c in range(n_blk):
            value = pg[inv[side * n_blk + c], 0:3, :]
            for a in range(3):
                row = a * n_blk + c
                piece = value[a : a + 1]
                if side == 1:
                    piece = piece + wf[row : row + 1, :]
                fsend[side, row : row + 1, :] = piece
    for index, (dp, dq) in enumerate(near_peers):
        send(fsend.at[1 + dp], frecv.at[index], 7, dp, dq)
    wait_bytes(frecv, rsem.at[7])
    force = fsend[1]
    for index in range(len(near_peers)):
        force = force + frecv[index]
    for a in range(3):
        for c in range(n_blk):
            row = a * n_blk + c
            out_ref[a : a + 1, c * bs : (c + 1) * bs] = -force[row : row + 1]

    wait_bytes(wide.at[pl.ds(0, 2 * n_blk)], ssem.at[0])
    wait_bytes(zwide.at[pl.ds(0, 3 * n_blk - 1)], ssem.at[1])
    wait_bytes(qbuf.at[pl.ds(0, n_k - 1)], ssem.at[2])
    wait_bytes(rsb, ssem.at[3])
    wait_bytes(agb.at[pl.ds(0, n_at - 1)], ssem.at[4])
    wait_bytes(cgr, ssem.at[5])
    wait_bytes(trecv, ssem.at[6])
    wait_bytes(frecv, ssem.at[7])


def body(
    n_at, n_k,
    positions, features, filter_one, filter_two, readout_in, readout_out, charge_weight,
    neighbour_blocks, live_slots, wave_ints,
):
    n_f = features.shape[0]
    n_m = filter_one.shape[0]
    n_q = charge_weight.shape[1]
    n_blk, n_slot = neighbour_blocks.shape
    bs = positions.shape[1] // n_blk
    n_wave = wave_ints.shape[1]
    local = n_blk * bs
    wide_n = n_slot * bs
    near_n = 3 * n_blk - 1
    k_chunks = n_wave // bs
    sizes = (n_at, n_k, n_blk, bs, n_slot, n_f, n_m, n_q, n_wave)
    v = pltpu.VMEM
    scratch = [
        v((3 * n_blk, n_f + 8, bs), f32),
        v((3 * n_blk, n_f, bs), f32),
        v((n_blk, bs, bs), f32),
        v((bs, bs), f32),
        v((bs, bs), f32),
        v((8, n_wave), f32),
        v((k_chunks, 8, bs), f32),
        v((2 * local, 2 * n_wave), bf16),
        v((4 * n_wave, local), bf16),
        v((2 * n_m * bs, wide_n), bf16),
        v((2 * wide_n, n_m * bs), bf16),
        v((4 * n_f, wide_n), bf16),
        v((4 * n_f, wide_n), bf16),
        v((7, bs, wide_n), f32),
        v((n_m, 2 * n_f), f32),
        v((n_m, 2 * n_f), f32),
        v((bs, bs), f32),
        v((bs, bs), f32),
        v((2 * n_f, n_m * bs), bf16),
        v((n_m * bs, 4 * n_f), bf16),
        v((n_m * 32, wide_n), f32),
        v((n_m * 32, wide_n), f32),
        v((bs, wide_n), f32),
        v((n_slot + 1, n_f, bs), f32),
        v((near_n, n_f, bs), f32),
        v((near_n, n_f, bs), f32),
        v((n_k, n_q, bs), f32),
        v((n_at, n_q, bs), f32),
        v((n_at - 1, n_q, bs), f32),
        v((n_at, n_q, bs), f32),
        v((n_q, bs), f32),
        v((n_at // n_group, 8 * n_q, n_group * bs), bf16),
        v((n_blk, n_q, bs), f32),
        v((n_k - 1, n_q, bs), f32),
        v((16, bs), f32),
        v((n_slot + 1, 8, bs), f32),
        v((3, 16, bs), f32),
        v((near_n, 16, bs), f32),
        pltpu.SMEM((3 * n_blk,), jnp.int32),
        pltpu.SemaphoreType.DMA((8,)),
        pltpu.SemaphoreType.DMA((8,)),
        pltpu.SemaphoreType.DMA((2,)),
        pltpu.SemaphoreType.DMA((n_at // n_group,)),
        pltpu.SemaphoreType.REGULAR((5,)),
    ]
    vmem = pl.BlockSpec(memory_space=pltpu.VMEM)
    smem = pl.BlockSpec(memory_space=pltpu.SMEM)
    return pl.pallas_call(
        functools.partial(kernel, sizes),
        out_shape=jax.ShapeDtypeStruct(positions.shape, f32),
        in_specs=[vmem] * 8 + [smem] * 2,
        out_specs=vmem,
        scratch_shapes=scratch,
        compiler_params=pltpu.CompilerParams(
            collective_id=0, has_side_effects=True, vmem_limit_bytes=56 * 2**20
        ),
    )(
        positions, features, filter_one, filter_two, readout_in,
        readout_out.reshape(1, n_f), charge_weight.T, wave_ints, neighbour_blocks, live_slots,
    )


def solution(mesh):
    in_specs = (
        P(None, "atoms"), P(None, "atoms"), P(), P(), P(), P(), P(),
        P("atoms", None), P("atoms"), P(None, "kvec"),
    )
    return jax.shard_map(
        functools.partial(body, mesh.shape["atoms"], mesh.shape["kvec"]),
        mesh=mesh, in_specs=in_specs, out_specs=P(None, "atoms"), check_vma=False,
    )
```
